128 devices in a mesh: dp: 2 (over y_lo), expert: 8 (over z, core), seq: 8 (over y_hi, x).
Axes of the slice: x: 4, y: 4 (y_hi: 2, y_lo: 2; y = y_hi * 2 + y_lo), z: 4, core: 2. Of those that a mesh axis runs over, the one named last changes fastest.
Arguments:
- attn_query: bfloat16 [32768, 2048], P(('dp', 'expert', 'seq')), may hold values from -5 to 5
- attn_key: bfloat16 [32768, 2048], P(('dp', 'expert', 'seq')), may hold values from -5 to 5
- attn_value: bfloat16 [32768, 2048], P(('dp', 'expert', 'seq')), may hold values from -5 to 5
- moe_input: bfloat16 [32768, 2048], P(('dp', 'expert', 'seq')), may hold values from -6 to 6
- cotangent: bfloat16 [32768, 2048], P(('dp', 'expert', 'seq')), may hold values from -6 to 6
- routes: int32 [32768, 2], P(('dp', 'expert', 'seq')), may hold values from 0 to 7, all different within a row; in each aligned block of 256 rows (0 to 255, 256 to 511, ...) at most 128 rows name the same one
- route_weight: bfloat16 [32768, 2], P(('dp', 'expert', 'seq')), may hold values from 0.099609375 to 1
- w_gate: bfloat16 [8, 2048, 512], P('expert'), may hold values from -0.125 to 0.125
- w_up: bfloat16 [8, 2048, 512], P('expert'), may hold values from -0.125 to 0.125
- w_down: bfloat16 [8, 512, 2048], P('expert'), may hold values from -0.25 to 0.25
Outputs:
- grad_hidden: bfloat16 [32768, 2048], P(('dp', 'expert', 'seq'))
- grad_query: bfloat16 [32768, 2048], P(('dp', 'expert', 'seq'))
- grad_key: bfloat16 [32768, 2048], P(('dp', 'expert', 'seq'))
- grad_value: bfloat16 [32768, 2048], P(('dp', 'expert', 'seq'))
- grad_gate: bfloat16 [8, 2048, 512], P('expert')
- grad_up: bfloat16 [8, 2048, 512], P('expert')
- grad_down: bfloat16 [8, 512, 2048], P('expert')
The draws below stay inside these ranges and needn't reach their ends.
Inputs may be any that keep to these rules, and one draw needn't show every extreme that they name: `routes`: in the rows of one device no expert is named by more than 128 rows; a row names 2 different experts.
All inputs are finite; a program needn't handle non-finite values.
Results may differ from the reference program's by a relative error of at most 0.02.
Values may be sent and summed in bfloat16 or wider, within the bound.
A program may use at most 192 MiB of HBM per device.

```python
import math
import jax
import jax.numpy as jnp
import numpy as np
from jax import lax

D = 2048
H = 16
FF = 512
TOK_DEV = 256
TOP = 2
HD = 128
EXPERTS = 8
MOST = 128
LEN = 2048
TOKENS = 32768
N_DP = 2
N_EXPERT = 8
N_SEQ = 8


def draw_attn_query(key, part):
    key = jax.random.fold_in(key, 11)
    base = jnp.clip(jax.random.normal(key, (TOKENS, D), jnp.float32), -5.0, 5.0)
    return base.astype(jnp.bfloat16)


def draw_attn_key(key, part):
    key = jax.random.fold_in(key, 23)
    base = jnp.clip(jax.random.normal(key, (TOKENS, D), jnp.float32), -5.0, 5.0)
    return base.astype(jnp.bfloat16)


def block_levels(rng, extent, split, smallest, high):
    def one(position, shards_of):
        draws = jax.random.uniform(jax.random.fold_in(jax.random.fold_in(rng, 6), position), (shards_of,), jnp.float32, smallest / len(split), high / len(split))
        return jnp.repeat(jnp.exp(draws), extent[position] // shards_of).reshape((-1,) + (1,) * (len(extent) - position - 1))

    gain = one(*split[0])
    for cut in split[1:]:
        gain = gain * one(*cut)
    return gain


def shared_out(stream_key, own, number, rows, amount, top, bound, skew):
    order = jax.random.permutation(stream_key, amount)
    crowded, common = shares(amount, rows * top, bound, skew, True), shares(amount, rows * top, bound, skew, False)
    places = jnp.arange(amount)

    def named(sizes, rotation):
        used = int((sizes > 0).sum())
        fixed = max(1, used // 4)
        passed = fixed + (places - fixed + rotation * (used - fixed)) % max(1, amount - fixed)
        return jnp.zeros((amount,), jnp.int32).at[order[jnp.where(places < fixed, places, passed)]].set(jnp.asarray(sizes, jnp.int32))

    sizes = jnp.where(number % 4 == 0, named(crowded, number // 4), named(common, number - number // 4 - 1))
    mixed = jax.random.permutation(jax.random.fold_in(own, 3), amount)
    source_of, taker = mixed[0:amount // 2 * 2:2], mixed[1:amount // 2 * 2:2]
    slack = jnp.minimum(sizes[source_of] - 1, bound - sizes[taker]) // 2
    slack = jnp.where((source_of == order[0]) | (taker == order[0]) | (sizes[taker] == 0), 0, jnp.maximum(slack, 0))
    passed = jax.random.randint(jax.random.fold_in(own, 4), (amount // 2,), 0, 1 << 20) % (slack + 1)
    sizes = sizes.at[source_of].add(-passed).at[taker].add(passed)
    items = jnp.searchsorted(jnp.cumsum(sizes), jnp.arange(rows * top), side="right").astype(jnp.int32)
    listing = items.reshape(top, rows).T
    listing = listing[jax.random.permutation(jax.random.fold_in(own, 1), rows)]
    rotation = jax.random.randint(jax.random.fold_in(own, 2), (rows, 1), 0, top)
    return jnp.take_along_axis(listing, (jnp.arange(top)[None, :] + rotation) % top, axis=1)


def shares(amount, total, reach, skew, full):
    portions = [(1 << 20) // math.isqrt(standing ** skew) + 1 for standing in range(1, amount + 1)]
    largest = reach if full else min(reach, max(-(-total // amount), total * portions[0] // sum(portions)))
    least = 1 if total - largest >= amount - 1 else 0
    given, surplus = [largest] + [least] * (amount - 1), total - largest - least * (amount - 1)
    while surplus > 0:
        free = [i for i in range(1, amount) if given[i] < largest] or [i for i in range(1, amount) if given[i] < reach]
        pool, left = sum([portions[i] for i in free]), surplus
        for i in free:
            extra = min(reach - given[i], max(1, left * portions[i] // pool), surplus)
            given[i] = given[i] + extra
            surplus = surplus - extra
    return np.array(given)


def noise(own_key, shape, spread, limit, split=(), kind=jnp.bfloat16):
    values = jax.random.normal(own_key, shape, jnp.float32) * spread
    if len(split) > 0:
        values = block_levels(own_key, shape, split, -0.22, 0.18) * values
    return jnp.clip(values, min=-limit, max=limit).astype(kind)


def setup_inputs(seed: int = 0) -> dict:
    splits = jax.random.split(jax.random.key(seed), 11)
    attn_query = draw_attn_query(jax.random.fold_in(splits[10], 71), 0)
    attn_key = draw_attn_key(jax.random.fold_in(splits[10], 71), 0)
    attn_value = noise(splits[2], (TOKENS, D), 1.0, 5.0, ((0, 128),))
    moe_input = noise(splits[3], (TOKENS, D), 1.0, 6.0, ((0, 128),))
    cotangent = noise(splits[4], (TOKENS, D), 1.0, 6.0, ((0, 128),))
    routes_keys = jax.random.split(jax.random.fold_in(splits[5], 1), TOKENS // TOK_DEV)
    routes_turns = jax.random.permutation(jax.random.fold_in(splits[5], 3), TOKENS // TOK_DEV)
    routes = jax.vmap(lambda own, number: shared_out(jax.random.fold_in(splits[5], 2), own, number, TOK_DEV, EXPERTS, TOP, MOST, 2))(routes_keys, routes_turns).reshape((TOKENS, TOP))
    route_weight = jnp.clip(0.099609375 + 0.9003906 * jax.random.uniform(splits[6], (TOKENS, TOP), jnp.float32) ** block_levels(splits[6], (TOKENS, TOP), ((0, 128),), -0.2, 0.2), 0.099609375, 1.0).astype(jnp.bfloat16)
    w_gate = noise(splits[7], (EXPERTS, D, FF), D ** -0.5, 0.125, ((0, 8),))
    w_up = noise(splits[8], (EXPERTS, D, FF), D ** -0.5, 0.125, ((0, 8),))
    w_down = noise(splits[9], (EXPERTS, FF, D), FF ** -0.5, 0.25, ((0, 8),))
    return dict(attn_query=attn_query, attn_key=attn_key, attn_value=attn_value, moe_input=moe_input, cotangent=cotangent, routes=routes, route_weight=route_weight, w_gate=w_gate, w_up=w_up, w_down=w_down)


def slot_index(taken_rows, weight_rows, most_slots):
    place_rank = (jnp.cumsum(taken_rows, axis=1) - 1).astype(jnp.int32)
    slot_ids = jnp.arange(most_slots, dtype=jnp.int32)
    matched = (place_rank[:, None, :] == slot_ids[None, :, None]) & (taken_rows[:, None, :] > 0)
    positions = jnp.arange(taken_rows.shape[1], dtype=jnp.int32)
    row_index = jnp.sum(jnp.where(matched, positions[None, None, :], 0), axis=2).astype(jnp.int32)
    slot_weight = jnp.sum(jnp.where(matched, weight_rows[:, None, :], jnp.float32(0.0)), axis=2)
    return row_index, slot_weight


def expert_backward(rows_in, slot_weight, rows_grad, gate_matrix, up_matrix, down_matrix):
    contract_last = (((1,), (1,)), ((), ()))
    contract_first = (((0,), (0,)), ((), ()))
    gate_value = jnp.dot(rows_in, gate_matrix, preferred_element_type=jnp.float32)
    up_value = jnp.dot(rows_in, up_matrix, preferred_element_type=jnp.float32)
    sigmoid_gate = jax.nn.sigmoid(gate_value)
    activated = gate_value * sigmoid_gate
    inner_value = (activated * up_value).astype(jnp.bfloat16)
    scaled_grad = (slot_weight[:, None] * rows_grad.astype(jnp.float32)).astype(jnp.bfloat16)
    grad_inner = lax.dot_general(scaled_grad, down_matrix, contract_last, preferred_element_type=jnp.float32)
    grad_gate_value = (grad_inner * up_value * sigmoid_gate * (1.0 + gate_value * (1.0 - sigmoid_gate))).astype(jnp.bfloat16)
    grad_up_value = (grad_inner * activated).astype(jnp.bfloat16)
    back_sum = lax.dot_general(grad_gate_value, gate_matrix, contract_last, preferred_element_type=jnp.float32)
    back_sum = back_sum + lax.dot_general(grad_up_value, up_matrix, contract_last, preferred_element_type=jnp.float32)
    hidden_part = back_sum.astype(jnp.bfloat16)
    gate_part = lax.dot_general(rows_in, grad_gate_value, contract_first, preferred_element_type=jnp.float32)
    up_part = lax.dot_general(rows_in, grad_up_value, contract_first, preferred_element_type=jnp.float32)
    down_part = lax.dot_general(inner_value, scaled_grad, contract_first, preferred_element_type=jnp.float32)
    return hidden_part, gate_part, up_part, down_part


def rounded(part_sum):
    return lax.optimization_barrier(part_sum.astype(jnp.bfloat16)).astype(jnp.float32)


def by_group(array):
    rest = array.shape[1:]
    shaped = array.reshape((N_DP, N_EXPERT, N_SEQ, TOK_DEV) + rest)
    moved = jnp.moveaxis(shaped, 2, 1)
    return moved.reshape((N_DP * N_SEQ, N_EXPERT, TOK_DEV) + rest)


def from_group(array):
    rest = array.shape[3:]
    shaped = array.reshape((N_DP, N_SEQ, N_EXPERT, TOK_DEV) + rest)
    moved = jnp.moveaxis(shaped, 1, 2)
    return moved.reshape((TOKENS,) + rest)


def head_grads(items):
    query_head, key_head, value_head, grad_head = items
    scale_factor = jnp.float32(HD ** -0.5)
    scores = jnp.dot(query_head, key_head.T, preferred_element_type=jnp.float32) * scale_factor
    probs = jax.nn.softmax(scores, axis=-1)
    probs_b = probs.astype(jnp.bfloat16)
    grad_value = jnp.dot(probs_b.T, grad_head, preferred_element_type=jnp.float32).astype(jnp.bfloat16)
    grad_probs = jnp.dot(grad_head, value_head.T, preferred_element_type=jnp.float32)
    delta_sum = jnp.sum(probs * grad_probs, axis=-1, keepdims=True)
    grad_scores = (probs * (grad_probs - delta_sum)).astype(jnp.bfloat16)
    grad_query = (jnp.dot(grad_scores, key_head, preferred_element_type=jnp.float32) * scale_factor).astype(jnp.bfloat16)
    grad_key = (jnp.dot(grad_scores.T, query_head, preferred_element_type=jnp.float32) * scale_factor).astype(jnp.bfloat16)
    return grad_query, grad_key, grad_value


def heads_of(array):
    shaped = array.reshape(N_DP * N_EXPERT, LEN, H, HD)
    return jnp.transpose(shaped, (0, 2, 1, 3)).reshape(N_DP * N_EXPERT * H, LEN, HD)


def tokens_of(array):
    shaped = array.reshape(N_DP * N_EXPERT, H, LEN, HD)
    return jnp.transpose(shaped, (0, 2, 1, 3)).reshape(TOKENS, D)


def reference(attn_query, attn_key, attn_value, moe_input, cotangent, routes, route_weight, w_gate, w_up, w_down):
    groups_n = N_DP * N_SEQ
    expert_ids = jnp.arange(EXPERTS, dtype=jnp.int32)
    hits = routes[:, :, None] == expert_ids[None, None, :]
    weight_table = jnp.sum(jnp.where(hits, route_weight.astype(jnp.float32)[:, :, None], jnp.float32(0.0)), axis=1)
    taken_table = jnp.sum(hits.astype(jnp.int32), axis=1).astype(jnp.int32)
    group_input = by_group(moe_input)
    group_grad = by_group(cotangent)
    group_weight = by_group(weight_table)
    group_taken = by_group(taken_table)
    sources = jnp.arange(N_EXPERT, dtype=jnp.int32)[:, None]

    def one_item(carry, item):
        hidden_acc, gate_acc, up_acc, down_acc = carry
        expert = item // groups_n
        group = item % groups_n
        taken_rows = group_taken[group][:, :, expert]
        weight_rows = group_weight[group][:, :, expert]
        row_index, slot_weight = slot_index(taken_rows, weight_rows, MOST)
        rows_in = group_input[group][sources, row_index].reshape(N_EXPERT * MOST, D)
        rows_grad = group_grad[group][sources, row_index].reshape(N_EXPERT * MOST, D)
        hidden_part, gate_part, up_part, down_part = expert_backward(
            rows_in, slot_weight.reshape(-1), rows_grad, w_gate[expert], w_up[expert], w_down[expert])
        hidden_acc = hidden_acc.at[group, sources, row_index].add(
            hidden_part.reshape(N_EXPERT, MOST, D).astype(jnp.float32))
        gate_acc = gate_acc.at[expert].add(rounded(gate_part))
        up_acc = up_acc.at[expert].add(rounded(up_part))
        down_acc = down_acc.at[expert].add(rounded(down_part))
        return (hidden_acc, gate_acc, up_acc, down_acc), None

    start = (jnp.zeros((groups_n, N_EXPERT, TOK_DEV, D), jnp.float32),
             jnp.zeros((EXPERTS, D, FF), jnp.float32),
             jnp.zeros((EXPERTS, D, FF), jnp.float32),
             jnp.zeros((EXPERTS, FF, D), jnp.float32))
    items = jnp.arange(EXPERTS * groups_n, dtype=jnp.int32)
    (hidden_acc, gate_acc, up_acc, down_acc), unused = lax.scan(one_item, start, items)
    grad_hidden = (cotangent.astype(jnp.float32) + from_group(hidden_acc)).astype(jnp.bfloat16)
    grad_gate = (gate_acc / jnp.float32(groups_n)).astype(jnp.bfloat16)
    grad_up = (up_acc / jnp.float32(groups_n)).astype(jnp.bfloat16)
    grad_down = (down_acc / jnp.float32(groups_n)).astype(jnp.bfloat16)
    grad_query, grad_key, grad_value = lax.map(
        head_grads, (heads_of(attn_query), heads_of(attn_key), heads_of(attn_value), heads_of(grad_hidden)))
    return (grad_hidden, tokens_of(grad_query), tokens_of(grad_key), tokens_of(grad_value),
            grad_gate, grad_up, grad_down)
```

```python
import functools
import math

import jax
import jax.numpy as jnp
from jax import lax
from jax.experimental import pallas as pl
from jax.experimental.pallas import tpu as pltpu
from jax.sharding import PartitionSpec as P

TOP = 2

HD = 128
KC = 256
NT = (((1,), (1,)), ((), ()))


def dot(a, b):
    return jnp.dot(a, b, preferred_element_type=jnp.float32)


def dot_nt(a, b):
    return lax.dot_general(a, b, NT, preferred_element_type=jnp.float32)


def attn_kernel(q_ref, do_ref, k_ref, v_ref, dq_ref, dk_ref, dv_ref, s_ref, dp_ref, e_ref, kt_ref, dk_acc, dv_acc):
    step = pl.program_id(1)
    steps = pl.num_programs(1)
    n = k_ref.shape[0]
    chunks = n // KC
    bq = q_ref.shape[0]
    scale = HD ** -0.5
    to_exp2 = scale * math.log2(math.e)

    @pl.when(step == 0)
    def _():
        dk_acc[...] = jnp.zeros_like(dk_acc)
        dv_acc[...] = jnp.zeros_like(dv_acc)
        kt_ref[...] = k_ref[...].T

    q = q_ref[...]
    do = do_ref[...]
    m = None
    for i in range(chunks):
        rows = pl.ds(i * KC, KC)
        s = dot_nt(k_ref[rows, :], q)
        s_ref[rows, :] = s
        top = jnp.max(s, axis=0, keepdims=True)
        m = top if m is None else jnp.maximum(m, top)
        dp_ref[rows, :] = dot_nt(v_ref[rows, :], do)
    total = jnp.zeros((1, bq), jnp.float32)
    delta = jnp.zeros((1, bq), jnp.float32)
    for i in range(chunks):
        rows = pl.ds(i * KC, KC)
        e = jnp.exp2((s_ref[rows, :] - m) * to_exp2)
        total += jnp.sum(e, axis=0, keepdims=True)
        delta += jnp.sum(e * dp_ref[rows, :], axis=0, keepdims=True)
        e_ref[rows, :] = e.astype(jnp.bfloat16)
    inv = 1.0 / total
    delta = delta * inv
    do_t = (do.astype(jnp.float32).T * inv).astype(jnp.bfloat16)
    q_t = (q.astype(jnp.float32).T * inv).astype(jnp.bfloat16)
    dq_t = jnp.zeros((HD, bq), jnp.float32)
    for i in range(chunks):
        rows = pl.ds(i * KC, KC)
        e = e_ref[rows, :]
        dv_acc[rows, :] += dot_nt(e, do_t)
        g = (e.astype(jnp.float32) * (dp_ref[rows, :] - delta)).astype(jnp.bfloat16)
        dk_acc[rows, :] += dot_nt(g, q_t)
        dq_t += dot(kt_ref[:, rows], g)
    dq_ref[...] = (dq_t * (inv * scale)).T.astype(jnp.bfloat16)

    @pl.when(step == steps - 1)
    def _():
        dk_ref[...] = (dk_acc[...] * scale).astype(jnp.bfloat16)
        dv_ref[...] = dv_acc[...].astype(jnp.bfloat16)


def attention(q, k, v, do, bq=512):
    n, width = q.shape
    heads = width // HD
    tile = pl.BlockSpec((bq, HD), lambda h, i: (i, h))
    whole = pl.BlockSpec((n, HD), lambda h, i: (0, h))
    out = jax.ShapeDtypeStruct((n, width), jnp.bfloat16)
    return pl.pallas_call(
        attn_kernel,
        grid=(heads, n // bq),
        in_specs=[tile, tile, whole, whole],
        out_specs=[tile, whole, whole],
        out_shape=[out, out, out],
        scratch_shapes=[
            pltpu.VMEM((n, bq), jnp.float32),
            pltpu.VMEM((n, bq), jnp.float32),
            pltpu.VMEM((n, bq), jnp.bfloat16),
            pltpu.VMEM((HD, n), jnp.bfloat16),
            pltpu.VMEM((n, HD), jnp.float32),
            pltpu.VMEM((n, HD), jnp.float32),
        ],
        compiler_params=pltpu.CompilerParams(vmem_limit_bytes=48 << 20),
        cost_estimate=pl.CostEstimate(flops=10 * n * n * width, bytes_accessed=14 * n * width, transcendentals=heads * n * n),
        name="attention",
    )(q, do, k, v)

MESH = pl.DeviceIdType.MESH
ANY = pl.BlockSpec(memory_space=pl.ANY)


def enter(targets):
    barrier = pltpu.get_barrier_semaphore()
    for target in targets:
        pl.semaphore_signal(barrier, inc=1, device_id=target, device_id_type=MESH)
    pl.semaphore_wait(barrier, len(targets))


def remote(src, dst, send_sem, recv_sem, target):
    return pltpu.make_async_remote_copy(
        src_ref=src,
        dst_ref=dst,
        send_sem=send_sem,
        recv_sem=recv_sem,
        device_id=target,
        device_id_type=MESH,
    )


def strip(index, size):
    return pl.ds(pl.multiple_of(index * size, size), size)


def start_to_heads(srcs, dsts, send_sem, recv_sem, local_sem):
    me = lax.axis_index("seq")
    copies = []
    for a, (src, dst) in enumerate(zip(srcs, dsts)):
        for d in range(1, 8):
            to = lax.rem(me + d, 8)
            copies.append(
                remote(
                    src.at[:, strip(to, 256)],
                    dst.at[strip(me, 256), :],
                    send_sem.at[a, d],
                    recv_sem.at[a, d],
                    {"seq": to},
                )
            )
            copies[-1].start()
        copies.append(
            pltpu.make_async_copy(
                src.at[:, strip(me, 256)], dst.at[strip(me, 256), :], local_sem.at[a]
            )
        )
        copies[-1].start()
    return copies


def start_to_tokens(srcs, dsts, send_sem, recv_sem, local_sem):
    me = lax.axis_index("seq")
    copies = []
    for a, (src, dst) in enumerate(zip(srcs, dsts)):
        for d in range(1, 8):
            to = lax.rem(me + d, 8)
            copies.append(
                remote(
                    src.at[strip(to, 256), :],
                    dst.at[:, strip(me, 256)],
                    send_sem.at[a, d],
                    recv_sem.at[a, d],
                    {"seq": to},
                )
            )
            copies[-1].start()
        copies.append(
            pltpu.make_async_copy(
                src.at[strip(me, 256), :], dst.at[:, strip(me, 256)], local_sem.at[a]
            )
        )
        copies[-1].start()
    return copies


def seq_peers():
    me = lax.axis_index("seq")
    return [{"seq": lax.rem(me + d, 8)} for d in range(1, 8)]


def swap_kernel(start, count, *refs):
    srcs, dsts, sems = refs[:count], refs[count : 2 * count], refs[2 * count :]
    enter(seq_peers())
    for copy in start(srcs, dsts, *sems):
        copy.wait()


def swap(start, arrays, shape, collective_id, name):
    count = len(arrays)
    return pl.pallas_call(
        functools.partial(swap_kernel, start, count),
        out_shape=[jax.ShapeDtypeStruct(shape, jnp.bfloat16)] * count,
        in_specs=[ANY] * count,
        out_specs=[ANY] * count,
        scratch_shapes=[
            pltpu.SemaphoreType.DMA((count, 8)),
            pltpu.SemaphoreType.DMA((count, 8)),
            pltpu.SemaphoreType.DMA((count,)),
        ],
        compiler_params=pltpu.CompilerParams(collective_id=collective_id, has_side_effects=True),
        name=name,
    )(*arrays)


def sibling(index):
    return index + 1 - 2 * lax.rem(index, 2)


def spread_kernel(
    x_ref, c_ref, t_ref, q_ref, k_ref, v_ref,
    all_x, all_c, all_t, head_q, head_k, head_v,
    send_sem, recv_sem, local_sem, t_send, t_recv, seq_send, seq_recv, seq_local,
):
    me = lax.axis_index("expert")
    right, left, across = [lax.rem(me + d, 8) for d in (2, 6, 4)]
    pair = sibling(me)
    enter([{"expert": lax.rem(me + d, 8)} for d in range(1, 8)] + seq_peers())
    srcs, outs = (x_ref, c_ref), (all_x, all_c)
    sends = []

    def piece(a, half, owner, mine, target, send_at, recv_at):
        rows = pl.ds(half * 128, 128)
        src = srcs[a].at[rows, :] if mine else outs[a].at[owner, rows, :]
        return remote(
            src,
            outs[a].at[owner, rows, :],
            send_sem.at[send_at],
            recv_sem.at[recv_at],
            {"expert": target},
        )

    def recv_index(kind, a, half):
        return kind * 4 + a * 2 + half

    def send(a, half, owner, mine, target, kind):
        copy = piece(a, half, owner, mine, target, len(sends), recv_index(kind, a, half))
        copy.start()
        sends.append(copy)

    def arrived(a, half, owner, kind):
        piece(a, half, owner, False, me, 0, recv_index(kind, a, half)).wait_recv()

    small = []
    for d in range(1, 8):
        to = lax.rem(me + d, 8)
        copy = remote(t_ref, all_t.at[me], t_send.at[d], t_recv.at[d], {"expert": to})
        copy.start()
        small.append(copy)
    for a in (0, 1):
        for half in (0, 1):
            send(a, half, me, True, right, 0)
            send(a, 1 - half, me, True, left, 1)
        for half in (0, 1):
            send(a, half, me, True, pair, 3)
    local = [
        pltpu.make_async_copy(x_ref, all_x.at[me], local_sem.at[0]),
        pltpu.make_async_copy(c_ref, all_c.at[me], local_sem.at[1]),
        pltpu.make_async_copy(t_ref, all_t.at[me], local_sem.at[2]),
    ]
    for copy in local:
        copy.start()
    heads = start_to_heads(
        (q_ref, k_ref, v_ref), (head_q, head_k, head_v), seq_send, seq_recv, seq_local
    )
    for a in (0, 1):
        arrived(a, 0, left, 0)
        send(a, 0, left, False, right, 2)
        send(a, 0, left, False, pair, 4)
        arrived(a, 1, right, 1)
        send(a, 1, right, False, left, 2)
        send(a, 1, right, False, pair, 5)
        arrived(a, 1, left, 0)
        send(a, 1, left, False, pair, 4)
        arrived(a, 0, right, 1)
        send(a, 0, right, False, pair, 5)
    for a in (0, 1):
        for half in (0, 1):
            arrived(a, half, across, 2)
            send(a, half, across, False, pair, 6)
    for a in (0, 1):
        for half in (0, 1):
            for kind, owner in ((3, me), (4, left), (5, right), (6, across)):
                arrived(a, half, sibling(owner), kind)
    for copy in sends:
        copy.wait_send()
    for copy in local + small + heads:
        copy.wait()


def spread(x, c, table, q, k, v):
    shapes = [(8, 256, 2048)] * 2 + [(8, 8, 256)] + [(2048, 256)] * 3
    types = [jnp.bfloat16] * 2 + [jnp.float32] + [jnp.bfloat16] * 3
    dma = pltpu.SemaphoreType.DMA
    return pl.pallas_call(
        spread_kernel,
        out_shape=[jax.ShapeDtypeStruct(s, t) for s, t in zip(shapes, types)],
        in_specs=[ANY] * 6,
        out_specs=[ANY] * 6,
        scratch_shapes=[
            dma((28,)), dma((28,)), dma((3,)), dma((8,)), dma((8,)), dma((3, 8)), dma((3, 8)), dma((3,)),
        ],
        compiler_params=pltpu.CompilerParams(collective_id=1, has_side_effects=True),
        name="spread",
    )(x, c, table, q, k, v)


def expert_backward(rows_in, scaled_grad, gate_matrix, up_matrix, down_matrix):
    first = (((0,), (0,)), ((), ()))
    gate_value = dot(rows_in, gate_matrix)
    up_value = dot(rows_in, up_matrix)
    sigmoid_gate = jax.nn.sigmoid(gate_value)
    activated = gate_value * sigmoid_gate
    inner_value = (activated * up_value).astype(jnp.bfloat16)
    grad_inner = dot_nt(scaled_grad, down_matrix)
    grad_gate_value = (
        grad_inner * up_value * sigmoid_gate * (1.0 + gate_value * (1.0 - sigmoid_gate))
    ).astype(jnp.bfloat16)
    grad_up_value = (grad_inner * activated).astype(jnp.bfloat16)
    hidden_part = dot_nt(grad_gate_value, gate_matrix) + dot_nt(grad_up_value, up_matrix)
    parts = [
        lax.dot_general(a, b, first, preferred_element_type=jnp.float32).astype(jnp.bfloat16)
        for a, b in (
            (rows_in, grad_gate_value),
            (rows_in, grad_up_value),
            (inner_value, scaled_grad),
        )
    ]
    return hidden_part.astype(jnp.bfloat16), parts


def shards(
    attn_query, attn_key, attn_value, moe_input, cotangent,
    routes, route_weight, w_gate, w_up, w_down,
):
    rows, width = moe_input.shape
    experts = lax.axis_size("expert")
    mine = lax.axis_index("expert")
    expert_ids = jnp.arange(experts, dtype=jnp.int32)
    hits = routes.T[:, None, :] == expert_ids[None, :, None]
    table = jnp.sum(
        jnp.where(hits, route_weight.astype(jnp.float32).T[:, None, :], 0.0), axis=0
    )
    all_x, all_c, all_t, head_q, head_k, head_v = spread(
        moe_input, cotangent, table, attn_query, attn_key, attn_value
    )
    own = lax.dynamic_slice_in_dim(all_t, mine, 1, 1)[:, 0]
    taken = own > 0.0
    rank = jnp.cumsum(taken.astype(jnp.int32), axis=1) - 1
    slot_ids = jnp.arange(128, dtype=jnp.int32)
    matched = (rank[:, None, :] == slot_ids[None, :, None]) & taken[:, None, :]
    pick = matched.astype(jnp.bfloat16)
    pick_weight = jnp.where(matched, own[:, None, :], 0.0).astype(jnp.bfloat16)
    rows_in = jnp.einsum("bst,btd->bsd", pick, all_x).reshape(-1, width)
    scaled_grad = jnp.einsum("bst,btd->bsd", pick_weight, all_c).reshape(-1, width)
    hidden_part, parts = expert_backward(rows_in, scaled_grad, w_gate[0], w_up[0], w_down[0])
    terms = jnp.einsum("bst,bsd->btd", pick, hidden_part.reshape(8, 128, width))
    routed_sum = lax.psum_scatter(
        terms.reshape(experts * rows, width), "expert", scatter_dimension=0, tiled=True
    ).astype(jnp.float32)
    grad_hidden = (cotangent.astype(jnp.float32) + routed_sum).astype(jnp.bfloat16)
    sums = [lax.psum(part, ("dp", "seq")).astype(jnp.float32) for part in parts]
    groups = jnp.float32(lax.axis_size("dp") * lax.axis_size("seq"))
    grads = [(total / groups)[None].astype(jnp.bfloat16) for total in sums]
    (head_grad,) = swap(start_to_heads, [grad_hidden], (2048, 256), 2, "grad_to_heads")
    backs = attention(head_q, head_k, head_v, head_grad)
    grad_query, grad_key, grad_value = swap(
        start_to_tokens, backs, (rows, width), 3, "grads_to_tokens"
    )
    return (grad_hidden, grad_query, grad_key, grad_value, *grads)


def solution(mesh):
    tokens = P(("dp", "expert", "seq"), None)
    weights = P("expert", None, None)
    return jax.shard_map(
        shards,
        mesh=mesh,
        in_specs=(tokens,) * 7 + (weights,) * 3,
        out_specs=(tokens,) * 4 + (weights,) * 3,
        check_vma=False,
    )
```

```python
import functools
import math

import jax
import jax.numpy as jnp
from jax import lax
from jax.experimental import pallas as pl
from jax.experimental.pallas import tpu as pltpu
from jax.sharding import PartitionSpec as P

TOP = 2

HD = 128
NT = (((1,), (1,)), ((), ()))


def dot(a, b):
    return jnp.dot(a, b, preferred_element_type=jnp.float32)


def dot_nt(a, b):
    return lax.dot_general(a, b, NT, preferred_element_type=jnp.float32)


MESH = pl.DeviceIdType.MESH
ANY = pl.BlockSpec(memory_space=pl.ANY)


def enter(targets):
    barrier = pltpu.get_barrier_semaphore()
    for target in targets:
        pl.semaphore_signal(barrier, inc=1, device_id=target, device_id_type=MESH)
    pl.semaphore_wait(barrier, len(targets))


def remote(src, dst, send_sem, recv_sem, target):
    return pltpu.make_async_remote_copy(
        src_ref=src,
        dst_ref=dst,
        send_sem=send_sem,
        recv_sem=recv_sem,
        device_id=target,
        device_id_type=MESH,
    )


def strip(index, size):
    return pl.ds(pl.multiple_of(index * size, size), size)


def start_to_heads(srcs, dsts, send_sem, recv_sem, local_sem):
    me = lax.axis_index("seq")
    copies = []
    for a, (src, dst) in enumerate(zip(srcs, dsts)):
        for d in range(1, 8):
            to = lax.rem(me + d, 8)
            copies.append(
                remote(
                    src.at[:, strip(to, 256)],
                    dst.at[strip(me, 256), :],
                    send_sem.at[a, d],
                    recv_sem.at[a, d],
                    {"seq": to},
                )
            )
            copies[-1].start()
        copies.append(
            pltpu.make_async_copy(
                src.at[:, strip(me, 256)], dst.at[strip(me, 256), :], local_sem.at[a]
            )
        )
        copies[-1].start()
    return copies


def seq_peers():
    me = lax.axis_index("seq")
    return [{"seq": lax.rem(me + d, 8)} for d in range(1, 8)]


def sibling(index):
    return index + 1 - 2 * lax.rem(index, 2)


def spread_kernel(
    x_ref, c_ref, t_ref, q_ref, k_ref, v_ref,
    all_x, all_c, all_t, head_q, head_k, head_v,
    send_sem, recv_sem, local_sem, t_send, t_recv, seq_send, seq_recv, seq_local,
):
    me = lax.axis_index("expert")
    right, left, across = [lax.rem(me + d, 8) for d in (2, 6, 4)]
    pair = sibling(me)
    enter([{"expert": lax.rem(me + d, 8)} for d in range(1, 8)] + seq_peers())
    srcs, outs = (x_ref, c_ref), (all_x, all_c)
    sends = []

    def piece(a, half, owner, mine, target, send_at, recv_at):
        rows = pl.ds(half * 128, 128)
        src = srcs[a].at[rows, :] if mine else outs[a].at[owner, rows, :]
        return remote(
            src,
            outs[a].at[owner, rows, :],
            send_sem.at[send_at],
            recv_sem.at[recv_at],
            {"expert": target},
        )

    def recv_index(kind, a, half):
        return kind * 4 + a * 2 + half

    def send(a, half, owner, mine, target, kind):
        copy = piece(a, half, owner, mine, target, len(sends), recv_index(kind, a, half))
        copy.start()
        sends.append(copy)

    def arrived(a, half, owner, kind):
        piece(a, half, owner, False, me, 0, recv_index(kind, a, half)).wait_recv()

    small = []
    for d in range(1, 8):
        to = lax.rem(me + d, 8)
        copy = remote(t_ref, all_t.at[me], t_send.at[d], t_recv.at[d], {"expert": to})
        copy.start()
        small.append(copy)
    for a in (0, 1):
        for half in (0, 1):
            send(a, half, me, True, right, 0)
            send(a, 1 - half, me, True, left, 1)
        for half in (0, 1):
            send(a, half, me, True, pair, 3)
    local = [
        pltpu.make_async_copy(x_ref, all_x.at[me], local_sem.at[0]),
        pltpu.make_async_copy(c_ref, all_c.at[me], local_sem.at[1]),
        pltpu.make_async_copy(t_ref, all_t.at[me], local_sem.at[2]),
    ]
    for copy in local:
        copy.start()
    heads = start_to_heads(
        (q_ref, k_ref, v_ref), (head_q, head_k, head_v), seq_send, seq_recv, seq_local
    )
    for a in (0, 1):
        arrived(a, 0, left, 0)
        send(a, 0, left, False, right, 2)
        send(a, 0, left, False, pair, 4)
        arrived(a, 1, right, 1)
        send(a, 1, right, False, left, 2)
        send(a, 1, right, False, pair, 5)
        arrived(a, 1, left, 0)
        send(a, 1, left, False, pair, 4)
        arrived(a, 0, right, 1)
        send(a, 0, right, False, pair, 5)
    for a in (0, 1):
        for half in (0, 1):
            arrived(a, half, across, 2)
            send(a, half, across, False, pair, 6)
    for a in (0, 1):
        for half in (0, 1):
            for kind, owner in ((3, me), (4, left), (5, right), (6, across)):
                arrived(a, half, sibling(owner), kind)
    for copy in sends:
        copy.wait_send()
    for copy in local + small + heads:
        copy.wait()


def spread(x, c, table, q, k, v):
    shapes = [(8, 256, 2048)] * 2 + [(8, 8, 256)] + [(2048, 256)] * 3
    types = [jnp.bfloat16] * 2 + [jnp.float32] + [jnp.bfloat16] * 3
    dma = pltpu.SemaphoreType.DMA
    return pl.pallas_call(
        spread_kernel,
        out_shape=[jax.ShapeDtypeStruct(s, t) for s, t in zip(shapes, types)],
        in_specs=[ANY] * 6,
        out_specs=[ANY] * 6,
        scratch_shapes=[
            dma((28,)), dma((28,)), dma((3,)), dma((8,)), dma((8,)), dma((3, 8)), dma((3, 8)), dma((3,)),
        ],
        compiler_params=pltpu.CompilerParams(collective_id=1, has_side_effects=True),
        name="spread",
    )(x, c, table, q, k, v)


def add_rows(out, terms, rows, step):
    @pl.loop(0, rows, step=step)
    def _(at):
        at = pl.multiple_of(at, step)
        total = None
        for ref, base in terms:
            value = ref[pl.ds(pl.multiple_of(base + at, step), step), :].astype(jnp.float32)
            total = value if total is None else total + value
        ref, base, factor = out
        if factor is not None:
            total = total * factor
        ref[pl.ds(pl.multiple_of(base + at, step), step), :] = total.astype(jnp.bfloat16)


def flip(index):
    return index + 1 - 2 * lax.rem(index, 2)


def forward_block(index, q, k, vt, s, e, ot, inv, qt):
    h = lax.div(index, 8)
    at = lax.rem(index, 8)
    cols = strip(at, 256)
    to_exp2 = (HD ** -0.5) * math.log2(math.e)
    query = q[h, cols, :]
    top = None
    for i in range(8):
        rows = pl.ds(i * 256, 256)
        score = dot_nt(k[h, rows, :], query)
        s[rows, :] = score
        peak = jnp.max(score, axis=0, keepdims=True)
        top = peak if top is None else jnp.maximum(top, peak)
    total = jnp.zeros((1, 256), jnp.float32)
    attended = jnp.zeros((HD, 256), jnp.float32)
    for i in range(8):
        rows = pl.ds(i * 256, 256)
        expo = jnp.exp2((s[rows, :] - top) * to_exp2)
        total += jnp.sum(expo, axis=0, keepdims=True)
        expo = expo.astype(jnp.bfloat16)
        e[h, rows, cols] = expo
        attended += dot(vt[h, :, rows], expo)
    scale = 1.0 / total
    ot[h, :, cols] = attended
    inv[h, :, cols] = scale
    qt[h, :, cols] = (query.astype(jnp.float32).T * scale).astype(jnp.bfloat16)


def mix_kernel(
    terms, cot, parts, hq, hk, hv,
    gh_out, dq_out, dk_out, dv_out, w_out,
    comb, sib, z1, z2, cbuf, gh, keep, wrecv, shard,
    q, k, v, do, kt, vt, s, e, ot, inv, qt, dot_t, dqt, g, back,
    load_sem, sib_send, sib_recv, z_send, z_recv, rs_send, rs_recv, ag_send, ag_recv,
    gh_send, gh_recv, gh_local, out_send, out_recv, out_local, store_sem,
):
    expert = lax.axis_index("expert")
    seq = lax.axis_index("seq")
    dp = lax.axis_index("dp")
    z, core = lax.div(expert, 2), lax.rem(expert, 2)
    far, near = lax.div(seq, 4), lax.rem(seq, 4)
    z_a, z_b = flip(z), 3 - z
    targets = [flip(z_b), z_a, z_b, z]
    to_pair = {"expert": z * 2 + 1 - core}
    to_a = {"expert": z_a * 2 + core}
    to_b = {"expert": z_b * 2 + core}
    hops = {
        "xa": ({"seq": far * 4 + flip(near)}, lax.rem(lax.div(near, 2) + lax.rem(near, 2), 2)),
        "xb": ({"seq": far * 4 + 3 - near}, lax.div(near, 2)),
        "ya": ({"dp": 1 - dp}, lax.rem(far + dp, 2)),
        "yb": ({"dp": 1 - dp, "seq": (1 - far) * 4 + near}, far),
    }
    orders = [
        ("xa", "xb", "ya", "yb"), ("xb", "xa", "yb", "ya"),
        ("ya", "yb", "xa", "xb"), ("yb", "ya", "xb", "xa"),
    ]
    enter([to_pair, to_a, to_b, hops["ya"][0], hops["yb"][0]] + seq_peers())

    sizes = (768, 384, 192, 96)
    lands = (0, 768, 1152, 1344)
    send_at, keep_at = [], []
    for p in range(4):
        base, sent, kept = 0, [], []
        for i in range(4):
            bit = hops[orders[p][i]][1]
            sent.append(base + (1 - bit) * sizes[i])
            base = base + bit * sizes[i]
            kept.append(base)
        send_at.append(sent)
        keep_at.append(kept)

    def span(start, size):
        return pl.ds(pl.multiple_of(start, 32), size)

    def rs_copy(p, i):
        if i == 0:
            src = parts.at[span(p * 1536 + send_at[p][0], 768), :]
        else:
            src = keep.at[p, span(send_at[p][i] - keep_at[p][0], sizes[i]), :]
        dst = wrecv.at[p, pl.ds(lands[i], sizes[i]), :]
        return remote(src, dst, rs_send.at[p, i], rs_recv.at[p, i], hops[orders[p][i]][0])

    def rs_step(i):
        for p in range(4):
            rs_copy(p, i - 1).wait_recv()
            rows = sizes[i - 1]
            at = keep_at[p][i - 1] - keep_at[p][0]
            if i < 4:
                add_rows(
                    (keep.at[p], at, None),
                    [(keep.at[p], at), (wrecv.at[p], lands[i - 1])], rows, 32,
                )
                rs_copy(p, i).start()
            else:
                add_rows(
                    (shard.at[p], 0, 1.0 / 16.0),
                    [(keep.at[p], at), (wrecv.at[p], lands[3])], rows, 32,
                )

    def ag_copy(p, i):
        hop = orders[p][3 - i]
        size = sizes[3 - i]
        rows = span(p * 1536 + keep_at[p][3 - i], size)
        src = shard.at[p] if i == 0 else w_out.at[rows, :]
        return remote(src, w_out.at[rows, :], ag_send.at[p, i], ag_recv.at[p, i], hops[hop][0])

    def store_shard(p):
        rows = span(p * 1536 + keep_at[p][3], 96)
        return pltpu.make_async_copy(shard.at[p], w_out.at[rows, :], store_sem.at[1 + p])

    def ag_step(i):
        for p in range(4):
            if i == 1:
                store_shard(p).wait()
            if i > 0:
                ag_copy(p, i - 1).wait_recv()
            if i < 4:
                ag_copy(p, i).start()

    sib_copies = []
    for i in range(4):
        copy = remote(
            terms.at[targets[i] * 2 + 1 - core], sib.at[i], sib_send.at[i], sib_recv.at[i], to_pair
        )
        copy.start()
        sib_copies.append(copy)
    for p in range(4):
        rs_copy(p, 0).start()
    comb_loads = [
        pltpu.make_async_copy(terms.at[targets[i] * 2 + core], comb.at[i], load_sem.at[i])
        for i in range(4)
    ]
    keep_loads = [
        pltpu.make_async_copy(
            parts.at[span(p * 1536 + keep_at[p][0], 768), :], keep.at[p], load_sem.at[4 + p]
        )
        for p in range(4)
    ]
    cot_load = pltpu.make_async_copy(cot, cbuf, load_sem.at[8])
    head_loads = []
    for n, (src, dst) in enumerate(((hq, q), (hk, k), (hv, v))):
        for h in range(2):
            head_loads.append(
                pltpu.make_async_copy(
                    src.at[:, pl.ds(h * HD, HD)], dst.at[h], load_sem.at[9 + 2 * n + h]
                )
            )
    for copy in comb_loads + head_loads + keep_loads + [cot_load]:
        copy.start()

    def z_copy(n):
        first, second = pl.ds(0, 128), pl.ds(128, 128)
        src, dst, target = (
            (comb.at[0, first, :], z1.at[0, 0], to_a),
            (comb.at[0, second, :], z1.at[1, 0], to_b),
            (comb.at[1, first, :], z1.at[0, 1], to_a),
            (comb.at[2, second, :], z1.at[1, 1], to_b),
            (comb.at[2, first, :], z2.at[0], to_b),
            (comb.at[1, second, :], z2.at[1], to_a),
        )[n]
        return remote(src, dst, z_send.at[n], z_recv.at[n], target)

    def pair_sum(i, base, rows):
        add_rows((comb.at[i], base, None), [(comb.at[i], base), (sib.at[i], base)], rows, 16)

    def forward(first, last):
        def body(index, carry):
            forward_block(index, q, k, vt, s, e, ot, inv, qt)
            return carry

        lax.fori_loop(first, last, body, 0)

    for copy in head_loads:
        copy.wait()
    for h in range(2):
        kt[h] = k[h].T
        vt[h] = v[h].T
    for i in range(3):
        comb_loads[i].wait()
        sib_copies[i].wait_recv()
        pair_sum(i, 0, 256)
        if i == 0:
            z_copy(0).start()
            z_copy(1).start()
        else:
            z_copy(i + 1).start()
    comb_loads[3].wait()
    cot_load.wait()
    sib_copies[3].wait_recv()
    forward(0, 4)
    for copy in keep_loads:
        copy.wait()
    rs_step(1)
    forward(4, 6)
    z_copy(0).wait_recv()
    add_rows((comb.at[2], 0, None), [(comb.at[2], 0), (z1.at[0, 0], 0)], 128, 16)
    z_copy(4).start()
    z_copy(1).wait_recv()
    add_rows((comb.at[1], 128, None), [(comb.at[1], 128), (z1.at[1, 0], 0)], 128, 16)
    z_copy(5).start()
    forward(6, 11)
    rs_step(2)
    forward(11, 13)
    rs_step(3)
    z_copy(2).wait_recv()
    z_copy(3).wait_recv()
    forward(13, 14)
    rs_step(4)
    for p in range(4):
        store_shard(p).start()
    ag_step(0)
    forward(14, 16)
    for p in range(2):
        z_copy(4 + p).wait_recv()
        add_rows(
            (gh, 128 * p, None),
            [(cbuf, 128 * p), (comb.at[3], 128 * p), (sib.at[3], 128 * p), (z1.at[p, 1], 0), (z2.at[p], 0)],
            128, 16,
        )
    gh_copies = []
    for d in range(1, 8):
        to = lax.rem(seq + d, 8)
        copy = remote(
            gh.at[:, strip(to, 256)], do.at[strip(seq, 256), :], gh_send.at[d], gh_recv.at[d], {"seq": to}
        )
        copy.start()
        gh_copies.append(copy)
    copy = pltpu.make_async_copy(gh.at[:, strip(seq, 256)], do.at[strip(seq, 256), :], gh_local)
    copy.start()
    gh_copies.append(copy)
    gh_store = pltpu.make_async_copy(gh, gh_out, store_sem.at[0])
    gh_store.start()
    ag_step(1)
    for copy in gh_copies[:7]:
        copy.wait_recv()
    gh_copies[7].wait()
    ag_step(2)

    scale = HD ** -0.5
    outs = (dq_out, dk_out, dv_out)

    def out_copy(h, n, d):
        to = lax.rem(seq + d, 8)
        return remote(
            back.at[n, h, strip(to, 256), :],
            outs[n].at[:, pl.ds(pl.multiple_of(seq * 256 + h * HD, HD), HD)],
            out_send.at[h, n, d],
            out_recv.at[h, n, d],
            {"seq": to},
        )

    def out_own(h, n):
        return pltpu.make_async_copy(
            back.at[n, h, strip(seq, 256), :],
            outs[n].at[:, pl.ds(pl.multiple_of(seq * 256 + h * HD, HD), HD)],
            out_local.at[h, n],
        )

    for h in range(2):
        head = pl.ds(h * HD, HD)
        norm = inv[h]
        grad_t = do[:, head].astype(jnp.float32).T
        delta = jnp.sum(grad_t * ot[h], axis=0, keepdims=True) * norm
        dot_t[...] = (grad_t * norm).astype(jnp.bfloat16)
        dqt[...] = jnp.zeros_like(dqt)

        def chunk(d, carry):
            at = lax.rem(seq + d, 8)
            rows = strip(at, 256)
            expo = e[h, rows, :]
            grad_probs = dot_nt(v[h, rows, :], do[:, head])
            g[...] = (expo.astype(jnp.float32) * (grad_probs - delta)).astype(jnp.bfloat16)
            back[2, h, rows, :] = dot_nt(expo, dot_t[...]).astype(jnp.bfloat16)
            back[1, h, rows, :] = (dot_nt(g[...], qt[h]) * scale).astype(jnp.bfloat16)
            dqt[...] += dot(kt[h, :, rows], g[...])

            @pl.when(d > 0)
            def _():
                out_copy(h, 1, d).start()
                out_copy(h, 2, d).start()

            return carry

        lax.fori_loop(0, 4, chunk, 0)
        if h == 0:
            ag_step(3)
        lax.fori_loop(4, 8, chunk, 0)
        back[0, h] = (dqt[...] * (norm * scale)).T.astype(jnp.bfloat16)
        for d in range(1, 8):
            out_copy(h, 0, d).start()
        for n in range(3):
            out_own(h, n).start()
    ag_step(4)

    for copy in sib_copies + gh_copies[:7]:
        copy.wait_send()
    for n in range(6):
        z_copy(n).wait_send()
    for p in range(4):
        for i in range(4):
            rs_copy(p, i).wait_send()
            ag_copy(p, i).wait_send()
    gh_store.wait()
    for h in range(2):
        for n in range(3):
            out_own(h, n).wait()
            for d in range(1, 8):
                out_copy(h, n, d).wait()


def mix(terms, cot, parts, head_q, head_k, head_v):
    dma = pltpu.SemaphoreType.DMA
    bf16, f32 = jnp.bfloat16, jnp.float32
    shapes = [(256, 2048)] * 4 + [(6144, 512)]
    return pl.pallas_call(
        mix_kernel,
        out_shape=[jax.ShapeDtypeStruct(shape, bf16) for shape in shapes],
        in_specs=[ANY] * 6,
        out_specs=[ANY] * 5,
        scratch_shapes=[
            pltpu.VMEM((4, 256, 2048), bf16),
            pltpu.VMEM((4, 256, 2048), bf16),
            pltpu.VMEM((2, 2, 128, 2048), bf16),
            pltpu.VMEM((2, 128, 2048), bf16),
            pltpu.VMEM((256, 2048), bf16),
            pltpu.VMEM((256, 2048), bf16),
            pltpu.VMEM((4, 768, 512), bf16),
            pltpu.VMEM((4, 1440, 512), bf16),
            pltpu.VMEM((4, 96, 512), bf16),
            pltpu.VMEM((2, 2048, HD), bf16),
            pltpu.VMEM((2, 2048, HD), bf16),
            pltpu.VMEM((2, 2048, HD), bf16),
            pltpu.VMEM((2048, 256), bf16),
            pltpu.VMEM((2, HD, 2048), bf16),
            pltpu.VMEM((2, HD, 2048), bf16),
            pltpu.VMEM((2048, 256), f32),
            pltpu.VMEM((2, 2048, 2048), bf16),
            pltpu.VMEM((2, HD, 2048), f32),
            pltpu.VMEM((2, 1, 2048), f32),
            pltpu.VMEM((2, HD, 2048), bf16),
            pltpu.VMEM((HD, 2048), bf16),
            pltpu.VMEM((HD, 2048), f32),
            pltpu.VMEM((256, 2048), bf16),
            pltpu.VMEM((3, 2, 2048, HD), bf16),
            dma((15,)), dma((4,)), dma((4,)), dma((6,)), dma((6,)),
            dma((4, 4)), dma((4, 4)), dma((4, 4)), dma((4, 4)),
            dma((8,)), dma((8,)), dma, dma((2, 3, 8)), dma((2, 3, 8)), dma((2, 3)), dma((5,)),
        ],
        compiler_params=pltpu.CompilerParams(
            collective_id=2, has_side_effects=True, vmem_limit_bytes=62 << 20
        ),
        name="mix",
    )(terms, cot, parts, head_q, head_k, head_v)


def expert_backward(rows_in, scaled_grad, gate_matrix, up_matrix, down_matrix):
    first = (((0,), (0,)), ((), ()))
    gate_value = dot(rows_in, gate_matrix)
    up_value = dot(rows_in, up_matrix)
    sigmoid_gate = jax.nn.sigmoid(gate_value)
    activated = gate_value * sigmoid_gate
    inner_value = (activated * up_value).astype(jnp.bfloat16)
    grad_inner = dot_nt(scaled_grad, down_matrix)
    grad_gate_value = (
        grad_inner * up_value * sigmoid_gate * (1.0 + gate_value * (1.0 - sigmoid_gate))
    ).astype(jnp.bfloat16)
    grad_up_value = (grad_inner * activated).astype(jnp.bfloat16)
    hidden_part = dot_nt(grad_gate_value, gate_matrix) + dot_nt(grad_up_value, up_matrix)
    parts = [
        lax.dot_general(a, b, first, preferred_element_type=jnp.float32).astype(jnp.bfloat16)
        for a, b in (
            (rows_in, grad_gate_value),
            (rows_in, grad_up_value),
            (inner_value, scaled_grad),
        )
    ]
    return hidden_part.astype(jnp.bfloat16), parts


def shards(
    attn_query, attn_key, attn_value, moe_input, cotangent,
    routes, route_weight, w_gate, w_up, w_down,
):
    rows, width = moe_input.shape
    experts = lax.axis_size("expert")
    mine = lax.axis_index("expert")
    expert_ids = jnp.arange(experts, dtype=jnp.int32)
    hits = routes.T[:, None, :] == expert_ids[None, :, None]
    table = jnp.sum(
        jnp.where(hits, route_weight.astype(jnp.float32).T[:, None, :], 0.0), axis=0
    )
    all_x, all_c, all_t, head_q, head_k, head_v = spread(
        moe_input, cotangent, table, attn_query, attn_key, attn_value
    )
    own = lax.dynamic_slice_in_dim(all_t, mine, 1, 1)[:, 0]
    taken = own > 0.0
    rank = jnp.cumsum(taken.astype(jnp.int32), axis=1) - 1
    slot_ids = jnp.arange(128, dtype=jnp.int32)
    matched = (rank[:, None, :] == slot_ids[None, :, None]) & taken[:, None, :]
    pick = matched.astype(jnp.bfloat16)
    pick_weight = jnp.where(matched, own[:, None, :], 0.0).astype(jnp.bfloat16)
    rows_in = jnp.einsum("bst,btd->bsd", pick, all_x).reshape(-1, width)
    scaled_grad = jnp.einsum("bst,btd->bsd", pick_weight, all_c).reshape(-1, width)
    hidden_part, parts = expert_backward(rows_in, scaled_grad, w_gate[0], w_up[0], w_down[0])
    terms = jnp.einsum("bst,bsd->btd", pick, hidden_part.reshape(8, 128, width))
    gate_part, up_part, down_part = parts
    down_rows = jnp.swapaxes(down_part.reshape(512, 4, 512), 0, 1).reshape(2048, 512)
    joined = jnp.concatenate([gate_part, up_part, down_rows], axis=0)
    grad_hidden, grad_query, grad_key, grad_value, sums = mix(
        terms, cotangent, joined, head_q, head_k, head_v
    )
    grad_gate, grad_up = sums[:2048], sums[2048:4096]
    grad_down = jnp.swapaxes(sums[4096:].reshape(4, 512, 512), 0, 1).reshape(512, 2048)
    grads = [grad[None] for grad in (grad_gate, grad_up, grad_down)]
    return (grad_hidden, grad_query, grad_key, grad_value, *grads)


def solution(mesh):
    tokens = P(("dp", "expert", "seq"), None)
    weights = P("expert", None, None)
    return jax.shard_map(
        shards,
        mesh=mesh,
        in_specs=(tokens,) * 7 + (weights,) * 3,
        out_specs=(tokens,) * 4 + (weights,) * 3,
        check_vma=False,
    )
```

```python
import functools
import math

import jax
import jax.numpy as jnp
from jax import lax
from jax.experimental import pallas as pl
from jax.experimental.pallas import tpu as pltpu
from jax.sharding import PartitionSpec as P

TOP = 2

HD = 128
NT = (((1,), (1,)), ((), ()))


def dot(a, b):
    return jnp.dot(a, b, preferred_element_type=jnp.float32)


def dot_nt(a, b):
    return lax.dot_general(a, b, NT, preferred_element_type=jnp.float32)


MESH = pl.DeviceIdType.MESH
ANY = pl.BlockSpec(memory_space=pl.ANY)


def enter(targets):
    barrier = pltpu.get_barrier_semaphore()
    for target in targets:
        pl.semaphore_signal(barrier, inc=1, device_id=target, device_id_type=MESH)
    pl.semaphore_wait(barrier, len(targets))


def remote(src, dst, send_sem, recv_sem, target):
    return pltpu.make_async_remote_copy(
        src_ref=src,
        dst_ref=dst,
        send_sem=send_sem,
        recv_sem=recv_sem,
        device_id=target,
        device_id_type=MESH,
    )


def strip(index, size):
    return pl.ds(pl.multiple_of(index * size, size), size)


def start_to_heads(srcs, dsts, send_sem, recv_sem, local_sem):
    me = lax.axis_index("seq")
    copies = []
    for a, (src, dst) in enumerate(zip(srcs, dsts)):
        for d in range(1, 8):
            to = lax.rem(me + d, 8)
            copies.append(
                remote(
                    src.at[:, strip(to, 256)],
                    dst.at[strip(me, 256), :],
                    send_sem.at[a, d],
                    recv_sem.at[a, d],
                    {"seq": to},
                )
            )
            copies[-1].start()
        copies.append(
            pltpu.make_async_copy(
                src.at[:, strip(me, 256)], dst.at[strip(me, 256), :], local_sem.at[a]
            )
        )
        copies[-1].start()
    return copies


def seq_peers():
    me = lax.axis_index("seq")
    return [{"seq": lax.rem(me + d, 8)} for d in range(1, 8)]


def sibling(index):
    return index + 1 - 2 * lax.rem(index, 2)


def dot_tn(a, b):
    return lax.dot_general(a, b, (((0,), (0,)), ((), ())), preferred_element_type=jnp.float32)


def experts_kernel(
    x_ref, c_ref, t_ref, q_ref, k_ref, v_ref, wg_ref, wu_ref, wd_ref,
    terms, parts, head_q, head_k, head_v,
    all_x, all_c, all_t, wg, wu, wd, own_weight, own_rank, pick, pick_weight, pick_t,
    rows_in, gate_value, up_value, scaled, inner, grad_gate, grad_up, hidden, stage, acc, joined,
    send_sem, recv_sem, load_sem, t_send, t_recv, seq_send, seq_recv, seq_local, stage_sem, part_sem,
):
    me = lax.axis_index("expert")
    right, left, across = [lax.rem(me + d, 8) for d in (2, 6, 4)]
    pair = sibling(me)
    enter([{"expert": lax.rem(me + d, 8)} for d in range(1, 8)] + seq_peers())
    srcs, outs = (x_ref, c_ref), (all_x, all_c)
    sends = []

    def piece(a, half, owner, mine, target, send_at, recv_at):
        rows = pl.ds(half * 128, 128)
        src = srcs[a].at[rows, :] if mine else outs[a].at[owner, rows, :]
        return remote(
            src,
            outs[a].at[owner, rows, :],
            send_sem.at[send_at],
            recv_sem.at[recv_at],
            {"expert": target},
        )

    def recv_index(kind, a, half):
        return kind * 4 + a * 2 + half

    def send(a, half, owner, mine, target, kind):
        copy = piece(a, half, owner, mine, target, len(sends), recv_index(kind, a, half))
        copy.start()
        sends.append(copy)

    def arrived(a, half, owner, kind):
        piece(a, half, owner, False, me, 0, recv_index(kind, a, half)).wait_recv()

    small = []
    for d in range(1, 8):
        to = lax.rem(me + d, 8)
        copy = remote(t_ref, all_t.at[me], t_send.at[d], t_recv.at[d], {"expert": to})
        copy.start()
        small.append(copy)
    for a in (0, 1):
        for half in (0, 1):
            send(a, half, me, True, pair, 3)
        for half in (0, 1):
            send(a, half, me, True, right, 0)
            send(a, 1 - half, me, True, left, 1)
    loads = [
        pltpu.make_async_copy(src, dst, load_sem.at[n])
        for n, (src, dst) in enumerate((
            (t_ref, all_t.at[me]), (x_ref, all_x.at[me]), (wg_ref.at[0], wg), (wu_ref.at[0], wu),
            (c_ref, all_c.at[me]), (wd_ref.at[0], wd),
        ))
    ]
    for copy in loads:
        copy.start()
    heads = start_to_heads(
        (q_ref, k_ref, v_ref), (head_q, head_k, head_v), seq_send, seq_recv, seq_local
    )

    loads[0].wait()
    for copy in small:
        copy.wait_recv()
    for b in range(8):
        own_weight[pl.ds(b, 1), :] = all_t[b, pl.ds(me, 1), :]
    before = lax.broadcasted_iota(jnp.int32, (256, 256), 0)
    after = lax.broadcasted_iota(jnp.int32, (256, 256), 1)
    upto = jnp.where(before <= after, 1.0, 0.0).astype(jnp.bfloat16)
    taken = jnp.where(own_weight[...] > 0.0, 1.0, 0.0).astype(jnp.bfloat16)
    own_rank[...] = dot(taken, upto) - 1.0

    def fill_picks(b, carry):
        weight = own_weight[pl.ds(b, 1), :]
        rank = own_rank[pl.ds(b, 1), :]
        slot = lax.broadcasted_iota(jnp.int32, (128, 256), 0).astype(jnp.float32)
        hit = (slot == rank) & (weight > 0.0)
        chosen = jnp.where(hit, 1.0, 0.0)
        pick[b] = chosen.astype(jnp.bfloat16)
        pick_weight[b] = jnp.where(hit, jnp.broadcast_to(weight, hit.shape), 0.0).astype(jnp.bfloat16)
        pick_t[b] = chosen.T.astype(jnp.bfloat16)
        return carry

    lax.fori_loop(0, 8, fill_picks, 0)

    def gather_rows(chooser, source, base, out):
        for i in range(2):
            block = base + i

            @pl.loop(0, 2048, step=512)
            def _(at):
                cols = pl.ds(pl.multiple_of(at, 512), 512)
                out[pl.ds(i * 128, 128), cols] = dot(chooser[block], source[block, :, cols]).astype(jnp.bfloat16)

    def first_half(n, chip):
        gather_rows(pick, all_x, chip * 2, rows_in.at[n])
        gate_value[n] = dot(rows_in[n], wg[...])
        up_value[n] = dot(rows_in[n], wu[...])

    def stage_copy(i, chip):
        return pltpu.make_async_copy(stage.at[i], terms.at[chip * 2 + i], stage_sem.at[i])

    def second_half(n, chip, previous):
        gather_rows(pick_weight, all_c, chip * 2, scaled)
        grad_inner = dot_nt(scaled[...], wd[...])
        gate, up = gate_value[n], up_value[n]
        sig = jax.nn.sigmoid(gate)
        active = gate * sig
        inner[...] = (active * up).astype(jnp.bfloat16)
        grad_gate[...] = (grad_inner * up * sig * (1.0 + gate * (1.0 - sig))).astype(jnp.bfloat16)
        grad_up[...] = (grad_inner * active).astype(jnp.bfloat16)

        @pl.loop(0, 2048, step=512)
        def _(at):
            cols = pl.ds(pl.multiple_of(at, 512), 512)
            hidden[:, cols] = (
                dot_nt(grad_gate[...], wg[cols, :]) + dot_nt(grad_up[...], wu[cols, :])
            ).astype(jnp.bfloat16)

        for i in range(2):
            if previous is not None:
                stage_copy(i, previous).wait()

            @pl.loop(0, 2048, step=512)
            def _(at):
                cols = pl.ds(pl.multiple_of(at, 512), 512)
                stage[i, :, cols] = dot(
                    pick_t[chip * 2 + i], hidden[pl.ds(i * 128, 128), cols]
                ).astype(jnp.bfloat16)

            stage_copy(i, chip).start()

        @pl.loop(0, 4)
        def _(j):
            cols = strip(j, 512)
            for m, (a, b) in enumerate((
                (rows_in.at[n, :, cols], grad_gate), (rows_in.at[n, :, cols], grad_up), (inner, scaled.at[:, cols]),
            )):
                rows = pl.ds(pl.multiple_of(m * 2048 + j * 512, 512), 512)
                value = dot_tn(a[...], b[...])
                if n == 0:
                    acc[rows, :] = value
                elif n < 3:
                    acc[rows, :] += value
                else:
                    joined[rows, :] = (acc[rows, :] + value).astype(jnp.bfloat16)
                    pltpu.make_async_copy(joined.at[rows, :], parts.at[rows, :], part_sem.at[m, j]).start()

    def pair_arrived(a, kind, owner):
        for half in (0, 1):
            arrived(a, half, sibling(owner), kind)

    def relay(a):
        arrived(a, 0, left, 0)
        send(a, 0, left, False, right, 2)
        send(a, 0, left, False, pair, 4)
        arrived(a, 1, right, 1)
        send(a, 1, right, False, left, 2)
        send(a, 1, right, False, pair, 5)
        arrived(a, 1, left, 0)
        send(a, 1, left, False, pair, 4)
        arrived(a, 0, right, 1)
        send(a, 0, right, False, pair, 5)

    def relay_last(a):
        for half in (0, 1):
            arrived(a, half, across, 2)
            send(a, half, across, False, pair, 6)

    chips = [lax.div(owner, 2) for owner in (me, left, right, across)]
    loads[1].wait()
    pair_arrived(0, 3, me)
    loads[2].wait()
    loads[3].wait()
    first_half(0, chips[0])
    loads[4].wait()
    pair_arrived(1, 3, me)
    loads[5].wait()
    second_half(0, chips[0], None)
    relay(0)
    pair_arrived(0, 4, left)
    first_half(1, chips[1])
    pair_arrived(0, 5, right)
    first_half(2, chips[2])
    relay(1)
    pair_arrived(1, 4, left)
    second_half(1, chips[1], chips[0])
    relay_last(0)
    pair_arrived(1, 5, right)
    second_half(2, chips[2], chips[1])
    pair_arrived(0, 6, across)
    first_half(3, chips[3])
    relay_last(1)
    pair_arrived(1, 6, across)
    second_half(3, chips[3], chips[2])
    for copy in sends + small:
        copy.wait_send()
    for copy in heads:
        copy.wait()
    for i in range(2):
        stage_copy(i, chips[3]).wait()
    for m in range(3):
        for j in range(4):
            rows = pl.ds(m * 2048 + j * 512, 512)
            pltpu.make_async_copy(joined.at[rows, :], parts.at[rows, :], part_sem.at[m, j]).wait()


def experts(x, c, table, q, k, v, w_gate, w_up, w_down):
    dma = pltpu.SemaphoreType.DMA
    bf16, f32 = jnp.bfloat16, jnp.float32
    shapes = [(8, 256, 2048), (6144, 512)] + [(2048, 256)] * 3
    vmem = [
        ((8, 256, 2048), bf16), ((8, 256, 2048), bf16), ((8, 8, 256), f32),
        ((2048, 512), bf16), ((2048, 512), bf16), ((512, 2048), bf16),
        ((8, 256), f32), ((8, 256), f32),
        ((8, 128, 256), bf16), ((8, 128, 256), bf16), ((8, 256, 128), bf16),
        ((4, 256, 2048), bf16), ((4, 256, 512), f32), ((4, 256, 512), f32),
        ((256, 2048), bf16), ((256, 512), bf16), ((256, 512), bf16), ((256, 512), bf16),
        ((256, 2048), bf16), ((2, 256, 2048), bf16), ((6144, 512), f32), ((6144, 512), bf16),
    ]
    return pl.pallas_call(
        experts_kernel,
        out_shape=[jax.ShapeDtypeStruct(shape, bf16) for shape in shapes],
        in_specs=[ANY] * 9,
        out_specs=[ANY] * 5,
        scratch_shapes=[pltpu.VMEM(*kind) for kind in vmem] + [
            dma((28,)), dma((28,)), dma((6,)), dma((8,)), dma((8,)),
            dma((3, 8)), dma((3, 8)), dma((3,)), dma((2,)), dma((3, 4)),
        ],
        compiler_params=pltpu.CompilerParams(
            collective_id=1, has_side_effects=True, vmem_limit_bytes=62 << 20
        ),
        name="experts",
    )(x, c, table, q, k, v, w_gate, w_up, w_down)


def add_rows(out, terms, rows, step):
    @pl.loop(0, rows, step=step)
    def _(at):
        at = pl.multiple_of(at, step)
        total = None
        for ref, base in terms:
            value = ref[pl.ds(pl.multiple_of(base + at, step), step), :].astype(jnp.float32)
            total = value if total is None else total + value
        ref, base, factor = out
        if factor is not None:
            total = total * factor
        ref[pl.ds(pl.multiple_of(base + at, step), step), :] = total.astype(jnp.bfloat16)


def flip(index):
    return index + 1 - 2 * lax.rem(index, 2)


def forward_block(index, q, k, vt, s, e, ot, inv, qt):
    h = lax.div(index, 8)
    at = lax.rem(index, 8)
    cols = strip(at, 256)
    to_exp2 = (HD ** -0.5) * math.log2(math.e)
    query = q[h, cols, :]
    top = None
    for i in range(8):
        rows = pl.ds(i * 256, 256)
        score = dot_nt(k[h, rows, :], query)
        s[rows, :] = score
        peak = jnp.max(score, axis=0, keepdims=True)
        top = peak if top is None else jnp.maximum(top, peak)
    total = jnp.zeros((1, 256), jnp.float32)
    attended = jnp.zeros((HD, 256), jnp.float32)
    for i in range(8):
        rows = pl.ds(i * 256, 256)
        expo = jnp.exp2((s[rows, :] - top) * to_exp2)
        total += jnp.sum(expo, axis=0, keepdims=True)
        expo = expo.astype(jnp.bfloat16)
        e[h, rows, cols] = expo
        attended += dot(vt[h, :, rows], expo)
    scale = 1.0 / total
    ot[h, :, cols] = attended
    inv[h, :, cols] = scale
    qt[h, :, cols] = (query.astype(jnp.float32).T * scale).astype(jnp.bfloat16)


def mix_kernel(
    terms, cot, parts, hq, hk, hv,
    gh_out, dq_out, dk_out, dv_out, w_out,
    comb, sib, z1, z2, cbuf, gh, keep, wrecv, shard,
    q, k, v, do, kt, vt, s, e, ot, inv, qt, dot_t, dqt, g, back,
    load_sem, sib_send, sib_recv, z_send, z_recv, rs_send, rs_recv, ag_send, ag_recv,
    gh_send, gh_recv, gh_local, out_send, out_recv, out_local, store_sem,
):
    expert = lax.axis_index("expert")
    seq = lax.axis_index("seq")
    dp = lax.axis_index("dp")
    z, core = lax.div(expert, 2), lax.rem(expert, 2)
    far, near = lax.div(seq, 4), lax.rem(seq, 4)
    z_a, z_b = flip(z), 3 - z
    targets = [flip(z_b), z_a, z_b, z]
    to_pair = {"expert": z * 2 + 1 - core}
    to_a = {"expert": z_a * 2 + core}
    to_b = {"expert": z_b * 2 + core}
    hops = {
        "xa": ({"seq": far * 4 + flip(near)}, lax.rem(lax.div(near, 2) + lax.rem(near, 2), 2)),
        "xb": ({"seq": far * 4 + 3 - near}, lax.div(near, 2)),
        "ya": ({"dp": 1 - dp}, lax.rem(far + dp, 2)),
        "yb": ({"dp": 1 - dp, "seq": (1 - far) * 4 + near}, far),
    }
    orders = [
        ("xa", "xb", "ya", "yb"), ("xb", "xa", "yb", "ya"),
        ("ya", "yb", "xa", "xb"), ("yb", "ya", "xb", "xa"),
    ]
    enter([to_pair, to_a, to_b, hops["ya"][0], hops["yb"][0]] + seq_peers())

    sizes = (768, 384, 192, 96)
    lands = (0, 768, 1152, 1344)
    send_at, keep_at = [], []
    for p in range(4):
        base, sent, kept = 0, [], []
        for i in range(4):
            bit = hops[orders[p][i]][1]
            sent.append(base + (1 - bit) * sizes[i])
            base = base + bit * sizes[i]
            kept.append(base)
        send_at.append(sent)
        keep_at.append(kept)

    def span(start, size):
        return pl.ds(pl.multiple_of(start, 32), size)

    def rs_copy(p, i):
        if i == 0:
            src = parts.at[span(p * 1536 + send_at[p][0], 768), :]
        else:
            src = keep.at[p, span(send_at[p][i] - keep_at[p][0], sizes[i]), :]
        dst = wrecv.at[p, pl.ds(lands[i], sizes[i]), :]
        return remote(src, dst, rs_send.at[p, i], rs_recv.at[p, i], hops[orders[p][i]][0])

    def rs_step(i):
        for p in range(4):
            rs_copy(p, i - 1).wait_recv()
            rows = sizes[i - 1]
            at = keep_at[p][i - 1] - keep_at[p][0]
            if i < 4:
                add_rows(
                    (keep.at[p], at, None),
                    [(keep.at[p], at), (wrecv.at[p], lands[i - 1])], rows, 32,
                )
                rs_copy(p, i).start()
            else:
                add_rows(
                    (shard.at[p], 0, 1.0 / 16.0),
                    [(keep.at[p], at), (wrecv.at[p], lands[3])], rows, 32,
                )

    def ag_copy(p, i):
        hop = orders[p][3 - i]
        size = sizes[3 - i]
        rows = span(p * 1536 + keep_at[p][3 - i], size)
        src = shard.at[p] if i == 0 else w_out.at[rows, :]
        return remote(src, w_out.at[rows, :], ag_send.at[p, i], ag_recv.at[p, i], hops[hop][0])

    def store_shard(p):
        rows = span(p * 1536 + keep_at[p][3], 96)
        return pltpu.make_async_copy(shard.at[p], w_out.at[rows, :], store_sem.at[1 + p])

    def ag_step(i):
        for p in range(4):
            if i == 1:
                store_shard(p).wait()
            if i > 0:
                ag_copy(p, i - 1).wait_recv()
            if i < 4:
                ag_copy(p, i).start()

    sib_copies = []
    for i in range(4):
        copy = remote(
            terms.at[targets[i] * 2 + 1 - core], sib.at[i], sib_send.at[i], sib_recv.at[i], to_pair
        )
        copy.start()
        sib_copies.append(copy)
    for p in range(4):
        rs_copy(p, 0).start()
    comb_loads = [
        pltpu.make_async_copy(terms.at[targets[i] * 2 + core], comb.at[i], load_sem.at[i])
        for i in range(4)
    ]
    keep_loads = [
        pltpu.make_async_copy(
            parts.at[span(p * 1536 + keep_at[p][0], 768), :], keep.at[p], load_sem.at[4 + p]
        )
        for p in range(4)
    ]
    cot_load = pltpu.make_async_copy(cot, cbuf, load_sem.at[8])
    head_loads = []
    for n, (src, dst) in enumerate(((hq, q), (hk, k), (hv, v))):
        for h in range(2):
            head_loads.append(
                pltpu.make_async_copy(
                    src.at[:, pl.ds(h * HD, HD)], dst.at[h], load_sem.at[9 + 2 * n + h]
                )
            )
    for copy in comb_loads + head_loads + keep_loads + [cot_load]:
        copy.start()

    def z_copy(n):
        first, second = pl.ds(0, 128), pl.ds(128, 128)
        src, dst, target = (
            (comb.at[0, first, :], z1.at[0, 0], to_a),
            (comb.at[0, second, :], z1.at[1, 0], to_b),
            (comb.at[1, first, :], z1.at[0, 1], to_a),
            (comb.at[2, second, :], z1.at[1, 1], to_b),
            (comb.at[2, first, :], z2.at[0], to_b),
            (comb.at[1, second, :], z2.at[1], to_a),
        )[n]
        return remote(src, dst, z_send.at[n], z_recv.at[n], target)

    def pair_sum(i, base, rows):
        add_rows((comb.at[i], base, None), [(comb.at[i], base), (sib.at[i], base)], rows, 16)

    def forward(first, last):
        def body(index, carry):
            forward_block(index, q, k, vt, s, e, ot, inv, qt)
            return carry

        lax.fori_loop(first, last, body, 0)

    for copy in head_loads:
        copy.wait()
    for h in range(2):
        kt[h] = k[h].T
        vt[h] = v[h].T
    for i in range(3):
        comb_loads[i].wait()
        sib_copies[i].wait_recv()
        pair_sum(i, 0, 256)
        if i == 0:
            z_copy(0).start()
            z_copy(1).start()
        else:
            z_copy(i + 1).start()
    comb_loads[3].wait()
    cot_load.wait()
    sib_copies[3].wait_recv()
    forward(0, 4)
    for copy in keep_loads:
        copy.wait()
    rs_step(1)
    forward(4, 6)
    z_copy(0).wait_recv()
    add_rows((comb.at[2], 0, None), [(comb.at[2], 0), (z1.at[0, 0], 0)], 128, 16)
    z_copy(4).start()
    z_copy(1).wait_recv()
    add_rows((comb.at[1], 128, None), [(comb.at[1], 128), (z1.at[1, 0], 0)], 128, 16)
    z_copy(5).start()
    forward(6, 11)
    rs_step(2)
    forward(11, 13)
    rs_step(3)
    z_copy(2).wait_recv()
    z_copy(3).wait_recv()
    forward(13, 14)
    rs_step(4)
    for p in range(4):
        store_shard(p).start()
    ag_step(0)
    forward(14, 16)
    for p in range(2):
        z_copy(4 + p).wait_recv()
        add_rows(
            (gh, 128 * p, None),
            [(cbuf, 128 * p), (comb.at[3], 128 * p), (sib.at[3], 128 * p), (z1.at[p, 1], 0), (z2.at[p], 0)],
            128, 16,
        )
    gh_copies = []
    for d in range(1, 8):
        to = lax.rem(seq + d, 8)
        copy = remote(
            gh.at[:, strip(to, 256)], do.at[strip(seq, 256), :], gh_send.at[d], gh_recv.at[d], {"seq": to}
        )
        copy.start()
        gh_copies.append(copy)
    copy = pltpu.make_async_copy(gh.at[:, strip(seq, 256)], do.at[strip(seq, 256), :], gh_local)
    copy.start()
    gh_copies.append(copy)
    gh_store = pltpu.make_async_copy(gh, gh_out, store_sem.at[0])
    gh_store.start()
    ag_step(1)
    for copy in gh_copies[:7]:
        copy.wait_recv()
    gh_copies[7].wait()
    ag_step(2)

    scale = HD ** -0.5
    outs = (dq_out, dk_out, dv_out)

    def out_copy(h, n, d):
        to = lax.rem(seq + d, 8)
        return remote(
            back.at[n, h, strip(to, 256), :],
            outs[n].at[:, pl.ds(pl.multiple_of(seq * 256 + h * HD, HD), HD)],
            out_send.at[h, n, d],
            out_recv.at[h, n, d],
            {"seq": to},
        )

    def out_own(h, n):
        return pltpu.make_async_copy(
            back.at[n, h, strip(seq, 256), :],
            outs[n].at[:, pl.ds(pl.multiple_of(seq * 256 + h * HD, HD), HD)],
            out_local.at[h, n],
        )

    for h in range(2):
        head = pl.ds(h * HD, HD)
        norm = inv[h]
        grad_t = do[:, head].astype(jnp.float32).T
        delta = jnp.sum(grad_t * ot[h], axis=0, keepdims=True) * norm
        dot_t[...] = (grad_t * norm).astype(jnp.bfloat16)
        dqt[...] = jnp.zeros_like(dqt)

        def chunk(d, carry):
            at = lax.rem(seq + d, 8)
            rows = strip(at, 256)
            expo = e[h, rows, :]
            grad_probs = dot_nt(v[h, rows, :], do[:, head])
            g[...] = (expo.astype(jnp.float32) * (grad_probs - delta)).astype(jnp.bfloat16)
            back[2, h, rows, :] = dot_nt(expo, dot_t[...]).astype(jnp.bfloat16)
            back[1, h, rows, :] = (dot_nt(g[...], qt[h]) * scale).astype(jnp.bfloat16)
            dqt[...] += dot(kt[h, :, rows], g[...])

            @pl.when(d > 0)
            def _():
                out_copy(h, 1, d).start()
                out_copy(h, 2, d).start()

            return carry

        lax.fori_loop(0, 4, chunk, 0)
        if h == 0:
            ag_step(3)
        lax.fori_loop(4, 8, chunk, 0)
        back[0, h] = (dqt[...] * (norm * scale)).T.astype(jnp.bfloat16)
        for d in range(1, 8):
            out_copy(h, 0, d).start()
        for n in range(3):
            out_own(h, n).start()
    ag_step(4)

    for copy in sib_copies + gh_copies[:7]:
        copy.wait_send()
    for n in range(6):
        z_copy(n).wait_send()
    for p in range(4):
        for i in range(4):
            rs_copy(p, i).wait_send()
            ag_copy(p, i).wait_send()
    gh_store.wait()
    for h in range(2):
        for n in range(3):
            out_own(h, n).wait()
            for d in range(1, 8):
                out_copy(h, n, d).wait()


def mix(terms, cot, parts, head_q, head_k, head_v):
    dma = pltpu.SemaphoreType.DMA
    bf16, f32 = jnp.bfloat16, jnp.float32
    shapes = [(256, 2048)] * 4 + [(6144, 512)]
    return pl.pallas_call(
        mix_kernel,
        out_shape=[jax.ShapeDtypeStruct(shape, bf16) for shape in shapes],
        in_specs=[ANY] * 6,
        out_specs=[ANY] * 5,
        scratch_shapes=[
            pltpu.VMEM((4, 256, 2048), bf16),
            pltpu.VMEM((4, 256, 2048), bf16),
            pltpu.VMEM((2, 2, 128, 2048), bf16),
            pltpu.VMEM((2, 128, 2048), bf16),
            pltpu.VMEM((256, 2048), bf16),
            pltpu.VMEM((256, 2048), bf16),
            pltpu.VMEM((4, 768, 512), bf16),
            pltpu.VMEM((4, 1440, 512), bf16),
            pltpu.VMEM((4, 96, 512), bf16),
            pltpu.VMEM((2, 2048, HD), bf16),
            pltpu.VMEM((2, 2048, HD), bf16),
            pltpu.VMEM((2, 2048, HD), bf16),
            pltpu.VMEM((2048, 256), bf16),
            pltpu.VMEM((2, HD, 2048), bf16),
            pltpu.VMEM((2, HD, 2048), bf16),
            pltpu.VMEM((2048, 256), f32),
            pltpu.VMEM((2, 2048, 2048), bf16),
            pltpu.VMEM((2, HD, 2048), f32),
            pltpu.VMEM((2, 1, 2048), f32),
            pltpu.VMEM((2, HD, 2048), bf16),
            pltpu.VMEM((HD, 2048), bf16),
            pltpu.VMEM((HD, 2048), f32),
            pltpu.VMEM((256, 2048), bf16),
            pltpu.VMEM((3, 2, 2048, HD), bf16),
            dma((15,)), dma((4,)), dma((4,)), dma((6,)), dma((6,)),
            dma((4, 4)), dma((4, 4)), dma((4, 4)), dma((4, 4)),
            dma((8,)), dma((8,)), dma, dma((2, 3, 8)), dma((2, 3, 8)), dma((2, 3)), dma((5,)),
        ],
        compiler_params=pltpu.CompilerParams(
            collective_id=2, has_side_effects=True, vmem_limit_bytes=62 << 20
        ),
        name="mix",
    )(terms, cot, parts, head_q, head_k, head_v)


def shards(
    attn_query, attn_key, attn_value, moe_input, cotangent,
    routes, route_weight, w_gate, w_up, w_down,
):
    expert_ids = jnp.arange(8, dtype=jnp.int32)
    hits = routes.T[:, None, :] == expert_ids[None, :, None]
    table = jnp.sum(
        jnp.where(hits, route_weight.astype(jnp.float32).T[:, None, :], 0.0), axis=0
    )
    terms, joined, head_q, head_k, head_v = experts(
        moe_input, cotangent, table, attn_query, attn_key, attn_value, w_gate, w_up, w_down
    )
    grad_hidden, grad_query, grad_key, grad_value, sums = mix(
        terms, cotangent, joined, head_q, head_k, head_v
    )
    grad_gate, grad_up = sums[:2048], sums[2048:4096]
    grad_down = jnp.swapaxes(sums[4096:].reshape(4, 512, 512), 0, 1).reshape(512, 2048)
    grads = [grad[None] for grad in (grad_gate, grad_up, grad_down)]
    return (grad_hidden, grad_query, grad_key, grad_value, *grads)


def solution(mesh):
    tokens = P(("dp", "expert", "seq"), None)
    weights = P("expert", None, None)
    return jax.shard_map(
        shards,
        mesh=mesh,
        in_specs=(tokens,) * 7 + (weights,) * 3,
        out_specs=(tokens,) * 4 + (weights,) * 3,
        check_vma=False,
    )
```

```python
import functools
import math

import jax
import jax.numpy as jnp
from jax import lax
from jax.experimental import pallas as pl
from jax.experimental.pallas import tpu as pltpu
from jax.sharding import PartitionSpec as P

TOP = 2

HD = 128
NT = (((1,), (1,)), ((), ()))


def dot(a, b):
    return jnp.dot(a, b, preferred_element_type=jnp.float32)


def dot_nt(a, b):
    return lax.dot_general(a, b, NT, preferred_element_type=jnp.float32)


MESH = pl.DeviceIdType.MESH
ANY = pl.BlockSpec(memory_space=pl.ANY)


def enter(targets):
    barrier = pltpu.get_barrier_semaphore()
    for target in targets:
        pl.semaphore_signal(barrier, inc=1, device_id=target, device_id_type=MESH)
    pl.semaphore_wait(barrier, len(targets))


def remote(src, dst, send_sem, recv_sem, target):
    return pltpu.make_async_remote_copy(
        src_ref=src,
        dst_ref=dst,
        send_sem=send_sem,
        recv_sem=recv_sem,
        device_id=target,
        device_id_type=MESH,
    )


def strip(index, size):
    return pl.ds(pl.multiple_of(index * size, size), size)


def start_to_heads(srcs, dsts, send_sem, recv_sem, local_sem):
    me = lax.axis_index("seq")
    copies = []
    for a, (src, dst) in enumerate(zip(srcs, dsts)):
        for d in range(1, 8):
            to = lax.rem(me + d, 8)
            copies.append(
                remote(
                    src.at[:, strip(to, 256)],
                    dst.at[strip(me, 256), :],
                    send_sem.at[a, d],
                    recv_sem.at[a, d],
                    {"seq": to},
                )
            )
            copies[-1].start()
        copies.append(
            pltpu.make_async_copy(
                src.at[:, strip(me, 256)], dst.at[strip(me, 256), :], local_sem.at[a]
            )
        )
        copies[-1].start()
    return copies


def seq_peers():
    me = lax.axis_index("seq")
    return [{"seq": lax.rem(me + d, 8)} for d in range(1, 8)]


def sibling(index):
    return index + 1 - 2 * lax.rem(index, 2)


def dot_tn(a, b):
    return lax.dot_general(a, b, (((0,), (0,)), ((), ())), preferred_element_type=jnp.float32)


def flip(index):
    return index + 1 - 2 * lax.rem(index, 2)


def add_rows(out, base, terms, rows, step=16):
    @pl.loop(0, rows, step=step)
    def _(at):
        total = None
        for ref, start in terms:
            value = ref[pl.ds(pl.multiple_of(start + at, step), step), :].astype(jnp.float32)
            total = value if total is None else total + value
        out[pl.ds(pl.multiple_of(base + at, step), step), :] = total.astype(jnp.bfloat16)


def layer_kernel(
    x_ref, c_ref, t_ref, q_ref, k_ref, v_ref, wg_ref, wu_ref, wd_ref,
    gh_out, dq_out, dk_out, dv_out, gate_out, up_out, down_out, head_q, head_k, head_v,
    tokens, all_t, wg, wu, wd, own_weight, own_rank, pick, pick_weight, pick_t,
    rows_in, values, scaled, inner, grad_gate, grad_up, hidden, stage, joined,
    sib, z1, z2, wrecv, shard, do, ot, inv, dot_t, dqt,
    send_sem, recv_sem, load_sem, t_send, t_recv, seq_send, seq_recv, seq_local,
    sib_send, sib_recv, z_send, z_recv, rs_send, rs_recv, ag_send, ag_recv,
    gh_send, gh_recv, gh_local, out_send, out_recv, out_local, store_sem, shard_sem,
):
    me = lax.axis_index("expert")
    seq = lax.axis_index("seq")
    dp = lax.axis_index("dp")
    z, core = lax.div(me, 2), lax.rem(me, 2)
    far, near = lax.div(seq, 4), lax.rem(seq, 4)
    right, left, across = [lax.rem(me + d, 8) for d in (2, 6, 4)]
    pair = sibling(me)
    z_a, z_b = flip(z), 3 - z
    to_pair = {"expert": pair}
    to_a = {"expert": z_a * 2 + core}
    to_b = {"expert": z_b * 2 + core}
    hops = {
        "xa": ({"seq": far * 4 + flip(near)}, lax.rem(lax.div(near, 2) + lax.rem(near, 2), 2)),
        "xb": ({"seq": far * 4 + 3 - near}, lax.div(near, 2)),
        "ya": ({"dp": 1 - dp}, lax.rem(far + dp, 2)),
        "yb": ({"dp": 1 - dp, "seq": (1 - far) * 4 + near}, far),
    }
    orders = [
        ("xa", "xb", "ya", "yb"), ("xb", "xa", "yb", "ya"),
        ("ya", "yb", "xa", "xb"), ("yb", "ya", "xb", "xa"),
    ]
    enter(
        [{"expert": lax.rem(me + d, 8)} for d in range(1, 8)]
        + seq_peers()
        + [hops["ya"][0], hops["yb"][0]]
    )
    srcs = (x_ref, c_ref)
    sends = []

    def piece(a, half, owner, mine, target, send_at, recv_at):
        rows = pl.ds(half * 128, 128)
        dst = tokens.at[a * 8 + owner, rows, :]
        src = srcs[a].at[rows, :] if mine else dst
        return remote(src, dst, send_sem.at[send_at], recv_sem.at[recv_at], {"expert": target})

    def recv_index(kind, a, half):
        return kind * 4 + a * 2 + half

    def send(a, half, owner, mine, target, kind):
        copy = piece(a, half, owner, mine, target, len(sends), recv_index(kind, a, half))
        copy.start()
        sends.append(copy)

    def arrived(a, half, owner, kind):
        piece(a, half, owner, False, me, 0, recv_index(kind, a, half)).wait_recv()

    small = []
    for d in range(1, 8):
        to = lax.rem(me + d, 8)
        copy = remote(t_ref, all_t.at[me], t_send.at[d], t_recv.at[d], {"expert": to})
        copy.start()
        small.append(copy)
    for a in (0, 1):
        for half in (0, 1):
            send(a, half, me, True, pair, 3)
        for half in (0, 1):
            send(a, half, me, True, right, 0)
            send(a, 1 - half, me, True, left, 1)
    loads = [
        pltpu.make_async_copy(src, dst, load_sem.at[n])
        for n, (src, dst) in enumerate((
            (t_ref, all_t.at[me]), (x_ref, tokens.at[me]), (wg_ref.at[0], wg), (wu_ref.at[0], wu),
            (c_ref, tokens.at[8 + me]), (wd_ref.at[0], wd),
        ))
    ]
    for copy in loads:
        copy.start()
    heads = start_to_heads(
        (q_ref, k_ref, v_ref), (head_q, head_k, head_v), seq_send, seq_recv, seq_local
    )

    loads[0].wait()
    for copy in small:
        copy.wait_recv()
    for b in range(8):
        own_weight[pl.ds(b, 1), :] = all_t[b, pl.ds(me, 1), :]
    before = lax.broadcasted_iota(jnp.int32, (256, 256), 0)
    after = lax.broadcasted_iota(jnp.int32, (256, 256), 1)
    upto = jnp.where(before <= after, 1.0, 0.0).astype(jnp.bfloat16)
    taken = jnp.where(own_weight[...] > 0.0, 1.0, 0.0).astype(jnp.bfloat16)
    own_rank[...] = dot(taken, upto) - 1.0

    def fill_picks(b, carry):
        weight = own_weight[pl.ds(b, 1), :]
        rank = own_rank[pl.ds(b, 1), :]
        slot = lax.broadcasted_iota(jnp.int32, (128, 256), 0).astype(jnp.float32)
        hit = (slot == rank) & (weight > 0.0)
        chosen = jnp.where(hit, 1.0, 0.0)
        pick[b] = chosen.astype(jnp.bfloat16)
        pick_weight[b] = jnp.where(hit, jnp.broadcast_to(weight, hit.shape), 0.0).astype(jnp.bfloat16)
        pick_t[b] = chosen.T.astype(jnp.bfloat16)
        return carry

    lax.fori_loop(0, 8, fill_picks, 0)

    sizes, lands = (8, 4, 2, 1), (0, 8, 12, 14)
    send_at, keep_at = [], []
    for p in range(4):
        base, sent, kept = 0, [], []
        for i in range(4):
            bit = hops[orders[p][i]][1]
            sent.append(base + (1 - bit) * sizes[i])
            base = base + bit * sizes[i]
            kept.append(base)
        send_at.append(sent)
        keep_at.append(kept)

    def rs_copy(p, i):
        return remote(
            joined.at[p, pl.ds(send_at[p][i], sizes[i])],
            wrecv.at[p, pl.ds(lands[i], sizes[i])],
            rs_send.at[p, i], rs_recv.at[p, i], hops[orders[p][i]][0],
        )

    def rs_step(i):
        for p in range(4):
            rs_copy(p, i - 1).wait_recv()
            at = keep_at[p][i - 1]
            if i < 4:
                def add(r, carry):
                    total = joined[p, at + r].astype(jnp.float32) + wrecv[p, lands[i - 1] + r].astype(jnp.float32)
                    joined[p, at + r] = total.astype(jnp.bfloat16)
                    return carry

                lax.fori_loop(0, sizes[i - 1], add, 0)
                rs_copy(p, i).start()
            else:
                total = joined[p, at].astype(jnp.float32) + wrecv[p, 14].astype(jnp.float32)
                shard[p] = (total * (1.0 / 16.0)).astype(jnp.bfloat16)

    def final_rows(p, i, m):
        start, rows = keep_at[p][3 - i] * 32, sizes[3 - i] * 32
        if m < 2:
            return (gate_out, up_out)[m].at[0, pl.ds(pl.multiple_of(p * 512 + start, 32), rows), :]
        return down_out.at[0, pl.ds(pl.multiple_of(start, 32), rows), pl.ds(p * 512, 512)]

    def ag_copy(p, i, m):
        dst = final_rows(p, i, m)
        src = shard.at[p, pl.ds(m * 32, 32), :] if i == 0 else dst
        return remote(src, dst, ag_send.at[p, i, m], ag_recv.at[p, i, m], hops[orders[p][3 - i]][0])

    def store_shard(p, m):
        return pltpu.make_async_copy(
            shard.at[p, pl.ds(m * 32, 32), :], final_rows(p, 0, m), shard_sem.at[p, m]
        )

    def ag_step(i):
        for p in range(4):
            for m in range(3):
                if i == 0:
                    store_shard(p, m).start()
                if i == 1:
                    store_shard(p, m).wait()
                if i > 0:
                    ag_copy(p, i - 1, m).wait_recv()
            for m in range(3):
                if i < 4:
                    ag_copy(p, i, m).start()

    def gather_rows(chooser, first, base, out):
        for i in range(2):
            block = base + i

            @pl.loop(0, 2048, step=512)
            def _(at):
                cols = pl.ds(pl.multiple_of(at, 512), 512)
                out[pl.ds(i * 128, 128), cols] = dot(
                    chooser[block], tokens[first + block, :, cols]
                ).astype(jnp.bfloat16)

    def first_half(n, chip):
        gather_rows(pick, 0, chip * 2, rows_in.at[n])
        values[n // 2 % 2 if n < 3 else 0, 0] = dot(rows_in[n], wg[...])
        values[n // 2 % 2 if n < 3 else 0, 1] = dot(rows_in[n], wu[...])

    def sib_copy(n):
        return remote(stage.at[n % 2], sib.at[n], sib_send.at[n], sib_recv.at[n], to_pair)

    def scatter_rows(chip, which, out):
        @pl.loop(0, 2048, step=512)
        def _(at):
            cols = pl.ds(pl.multiple_of(at, 512), 512)
            out[:, cols] = dot(
                pick_t[chip * 2 + which], hidden[pl.ds(pl.multiple_of(which * 128, 128), 128), cols]
            ).astype(jnp.bfloat16)

    def weight_part(n, j):
        cols = strip(j, 512)
        for m, (a, b) in enumerate((
            (rows_in.at[n, :, cols], grad_gate), (rows_in.at[n, :, cols], grad_up), (inner, scaled.at[:, cols]),
        )):
            rows = pl.ds(m * 32, 32)
            value = dot_tn(a[...], b[...]).reshape(16, 32, 512)
            if n > 0:
                value += joined[j, :, rows, :].astype(jnp.float32)
            joined[j, :, rows, :] = value.astype(jnp.bfloat16)

    def second_half(n, chip):
        gather_rows(pick_weight, 8, chip * 2, scaled)
        grad_inner = dot_nt(scaled[...], wd[...])
        slot = 1 if n == 2 else 0
        gate, up = values[slot, 0], values[slot, 1]
        sig = jax.nn.sigmoid(gate)
        active = gate * sig
        inner[...] = (active * up).astype(jnp.bfloat16)
        grad_gate[...] = (grad_inner * up * sig * (1.0 + gate * (1.0 - sig))).astype(jnp.bfloat16)
        grad_up[...] = (grad_inner * active).astype(jnp.bfloat16)

        @pl.loop(0, 2048, step=512)
        def _(at):
            cols = pl.ds(pl.multiple_of(at, 512), 512)
            hidden[:, cols] = (
                dot_nt(grad_gate[...], wg[cols, :]) + dot_nt(grad_up[...], wu[cols, :])
            ).astype(jnp.bfloat16)

        if n >= 2:
            sib_copy(n - 2).wait_send()
        scatter_rows(chip, 1 - core, stage.at[n % 2])
        sib_copy(n).start()
        if n < 3:
            @pl.loop(0, 4)
            def _(j):
                weight_part(n, j)
        else:
            for j in range(4):
                weight_part(n, j)
                rs_copy(j, 0).start()
        scatter_rows(chip, core, rows_in.at[n])

    def pair_arrived(a, kind, owner):
        for half in (0, 1):
            arrived(a, half, sibling(owner), kind)

    def relay(a):
        arrived(a, 0, left, 0)
        send(a, 0, left, False, right, 2)
        send(a, 0, left, False, pair, 4)
        arrived(a, 1, right, 1)
        send(a, 1, right, False, left, 2)
        send(a, 1, right, False, pair, 5)
        arrived(a, 1, left, 0)
        send(a, 1, left, False, pair, 4)
        arrived(a, 0, right, 1)
        send(a, 0, right, False, pair, 5)

    def relay_last(a):
        for half in (0, 1):
            arrived(a, half, across, 2)
            send(a, half, across, False, pair, 6)

    def z_copy(n):
        first, second = pl.ds(0, 128), pl.ds(128, 128)
        src, dst, target = (
            (rows_in.at[3, first, :], z1.at[0, 0], to_a),
            (rows_in.at[3, second, :], z1.at[1, 0], to_b),
            (rows_in.at[1, first, :], z1.at[0, 1], to_a),
            (rows_in.at[2, second, :], z1.at[1, 1], to_b),
            (rows_in.at[2, first, :], z2.at[0], to_b),
            (rows_in.at[1, second, :], z2.at[1], to_a),
        )[n]
        return remote(src, dst, z_send.at[n], z_recv.at[n], target)

    def pair_sum(n):
        sib_copy(n).wait_recv()
        add_rows(rows_in.at[n], 0, [(rows_in.at[n], 0), (sib.at[n], 0)], 256)

    owner_a, owner_b = z_a * 2 + core, z_b * 2 + core
    kind_a = 5 - lax.rem(z, 2)
    kind_b = 9 - kind_a
    loads[1].wait()
    pair_arrived(0, 3, me)
    loads[2].wait()
    loads[3].wait()
    first_half(0, z)
    loads[4].wait()
    pair_arrived(1, 3, me)
    loads[5].wait()
    second_half(0, z)
    relay(0)
    pair_arrived(0, kind_a, owner_a)
    first_half(1, z_a)
    pair_arrived(0, kind_b, owner_b)
    first_half(2, z_b)
    relay(1)
    pair_arrived(1, kind_a, owner_a)
    second_half(1, z_a)
    relay_last(0)
    pair_arrived(1, kind_b, owner_b)
    second_half(2, z_b)
    pair_arrived(0, 6, across)
    first_half(3, lax.div(across, 2))
    pair_sum(1)
    z_copy(2).start()
    pair_sum(2)
    z_copy(3).start()
    relay_last(1)
    pair_arrived(1, 6, across)
    second_half(3, lax.div(across, 2))

    for copy in heads:
        copy.wait()
    head_loads = []
    for n, (src, dst, at) in enumerate(((head_q, wg, 0), (head_k, wg, 256), (head_v, wu, 0))):
        head_loads.append(
            pltpu.make_async_copy(src, dst.at[:, pl.ds(at, 256)], load_sem.at[6 + n])
        )
    cot_load = pltpu.make_async_copy(c_ref, scaled, load_sem.at[9])
    for copy in head_loads + [cot_load]:
        copy.start()
    pair_sum(3)
    z_copy(0).start()
    z_copy(1).start()
    for copy in sends + small:
        copy.wait_send()
    for copy in head_loads:
        copy.wait()

    def lanes(h):
        return pl.ds(pl.multiple_of(h * HD, HD), HD)

    def key_lanes(h):
        return pl.ds(pl.multiple_of(256 + h * HD, HD), HD)

    for h in range(2):
        wd[lanes(h), :] = wu[:, lanes(h)].T

    def forward_block(index, carry):
        h, at = lax.div(index, 8), lax.rem(index, 8)
        cols = strip(at, 256)
        to_exp2 = (HD ** -0.5) * math.log2(math.e)
        query = wg[cols, lanes(h)]
        top = None
        for i in range(8):
            score = dot_nt(wg[pl.ds(i * 256, 256), key_lanes(h)], query)
            values[i // 4, i // 2 % 2, :, pl.ds(i % 2 * 256, 256)] = score
            peak = jnp.max(score, axis=0, keepdims=True)
            top = peak if top is None else jnp.maximum(top, peak)
        total = jnp.zeros((1, 256), jnp.float32)
        attended = jnp.zeros((HD, 256), jnp.float32)
        for i in range(8):
            score = values[i // 4, i // 2 % 2, :, pl.ds(i % 2 * 256, 256)]
            expo = jnp.exp2((score - top) * to_exp2)
            total += jnp.sum(expo, axis=0, keepdims=True)
            expo = expo.astype(jnp.bfloat16)
            tokens[h * 8 + i, :, cols] = expo
            attended += dot(wd[lanes(h), pl.ds(i * 256, 256)], expo)
        scale = 1.0 / total
        ot[h, :, cols] = attended
        inv[h, :, cols] = scale
        wd[key_lanes(h), cols] = (query.astype(jnp.float32).T * scale).astype(jnp.bfloat16)
        return carry

    def forward(first, last):
        lax.fori_loop(first, last, forward_block, 0)

    forward(0, 6)
    rs_step(1)
    z_copy(0).wait_recv()
    add_rows(rows_in.at[2], 0, [(rows_in.at[2], 0), (z1.at[0, 0], 0)], 128)
    z_copy(4).start()
    z_copy(1).wait_recv()
    add_rows(rows_in.at[1], 128, [(rows_in.at[1], 128), (z1.at[1, 0], 0)], 128)
    z_copy(5).start()
    forward(6, 10)
    rs_step(2)
    forward(10, 12)
    rs_step(3)
    forward(12, 13)
    rs_step(4)
    ag_step(0)
    forward(13, 16)
    cot_load.wait()
    sib_copy(0).wait_recv()
    sib_copy(2).wait_send()
    gh = stage.at[0]
    for p in range(2):
        z_copy(2 + p).wait_recv()
        z_copy(4 + p).wait_recv()
        add_rows(
            gh, 128 * p,
            [
                (scaled, 128 * p), (rows_in.at[0], 128 * p), (sib.at[0], 128 * p),
                (z1.at[p, 1], 0), (z2.at[p], 0),
            ],
            128,
        )
    gh_copies = []
    for d in range(1, 8):
        to = lax.rem(seq + d, 8)
        copy = remote(
            gh.at[:, strip(to, 256)], do.at[strip(seq, 256), :], gh_send.at[d], gh_recv.at[d], {"seq": to}
        )
        copy.start()
        gh_copies.append(copy)
    gh_own = pltpu.make_async_copy(gh.at[:, strip(seq, 256)], do.at[strip(seq, 256), :], gh_local)
    gh_own.start()
    gh_store = pltpu.make_async_copy(gh, gh_out, store_sem)
    gh_store.start()
    ag_step(1)
    for h in range(2):
        wd[lanes(h), :] = wg[:, key_lanes(h)].T
    for copy in gh_copies:
        copy.wait_recv()
    gh_own.wait()
    ag_step(2)

    scale = HD ** -0.5
    outs = (dq_out, dk_out, dv_out)

    def back(n, h, rows):
        return (wg, wg, wu)[n].at[rows, key_lanes(h) if n == 1 else lanes(h)]

    def out_copy(h, n, d):
        to = lax.rem(seq + d, 8)
        return remote(
            back(n, h, strip(to, 256)), outs[n].at[:, lanes(seq * 2 + h)],
            out_send.at[h, n, d], out_recv.at[h, n, d], {"seq": to},
        )

    def out_own(h, n):
        return pltpu.make_async_copy(
            back(n, h, strip(seq, 256)), outs[n].at[:, lanes(seq * 2 + h)], out_local.at[h, n]
        )

    for h in range(2):
        head = pl.ds(h * HD, HD)
        norm = inv[h]
        grad_t = do[:, head].astype(jnp.float32).T
        delta = jnp.sum(grad_t * ot[h], axis=0, keepdims=True) * norm
        dot_t[...] = (grad_t * norm).astype(jnp.bfloat16)
        dqt[...] = jnp.zeros_like(dqt)

        def chunk(d, carry):
            at = lax.rem(seq + d, 8)
            rows = strip(at, 256)
            expo = tokens[h * 8 + at]
            grad_probs = dot_nt(wu[rows, head], do[:, head])
            hidden[...] = (expo.astype(jnp.float32) * (grad_probs - delta)).astype(jnp.bfloat16)
            wu[rows, head] = dot_nt(expo, dot_t[...]).astype(jnp.bfloat16)
            wg[rows, key_lanes(h)] = (dot_nt(hidden[...], wd[key_lanes(h), :]) * scale).astype(jnp.bfloat16)
            dqt[...] += dot(wd[lanes(h), rows], hidden[...])

            @pl.when(d > 0)
            def _():
                out_copy(h, 1, d).start()
                out_copy(h, 2, d).start()

            return carry

        lax.fori_loop(0, 4, chunk, 0)
        if h == 0:
            ag_step(3)
        lax.fori_loop(4, 8, chunk, 0)
        wg[:, head] = (dqt[...] * (norm * scale)).T.astype(jnp.bfloat16)
        for d in range(1, 8):
            out_copy(h, 0, d).start()
        for n in range(3):
            out_own(h, n).start()
    ag_step(4)

    sib_copy(3).wait_send()
    for copy in gh_copies:
        copy.wait_send()
    for n in range(6):
        z_copy(n).wait_send()
    for p in range(4):
        for i in range(4):
            rs_copy(p, i).wait_send()
            for m in range(3):
                ag_copy(p, i, m).wait_send()
    gh_store.wait()
    for h in range(2):
        for n in range(3):
            out_own(h, n).wait()
            for d in range(1, 8):
                out_copy(h, n, d).wait()


def layer(*arrays):
    dma = pltpu.SemaphoreType.DMA
    bf16, f32 = jnp.bfloat16, jnp.float32
    shapes = [(256, 2048)] * 4 + [(1, 2048, 512)] * 2 + [(1, 512, 2048)] + [(2048, 256)] * 3
    vmem = [
        ((16, 256, 2048), bf16), ((8, 8, 256), f32),
        ((2048, 512), bf16), ((2048, 512), bf16), ((512, 2048), bf16),
        ((8, 256), f32), ((8, 256), f32),
        ((8, 128, 256), bf16), ((8, 128, 256), bf16), ((8, 256, 128), bf16),
        ((4, 256, 2048), bf16), ((2, 2, 256, 512), f32),
        ((256, 2048), bf16), ((256, 512), bf16), ((256, 512), bf16), ((256, 512), bf16),
        ((256, 2048), bf16), ((2, 256, 2048), bf16), ((4, 16, 96, 512), bf16),
        ((4, 256, 2048), bf16), ((2, 2, 128, 2048), bf16), ((2, 128, 2048), bf16),
        ((4, 15, 96, 512), bf16), ((4, 96, 512), bf16), ((2048, 256), bf16),
        ((2, HD, 2048), f32), ((2, 1, 2048), f32), ((HD, 2048), bf16), ((HD, 2048), f32),
    ]
    sems = [
        (28,), (28,), (10,), (8,), (8,), (3, 8), (3, 8), (3,),
        (4,), (4,), (6,), (6,), (4, 4), (4, 4), (4, 4, 3), (4, 4, 3),
        (8,), (8,), (), (2, 3, 8), (2, 3, 8), (2, 3), (), (4, 3),
    ]
    return pl.pallas_call(
        layer_kernel,
        out_shape=[jax.ShapeDtypeStruct(shape, bf16) for shape in shapes],
        in_specs=[ANY] * len(arrays),
        out_specs=[ANY] * len(shapes),
        scratch_shapes=[pltpu.VMEM(*kind) for kind in vmem] + [dma(s) if s else dma for s in sems],
        compiler_params=pltpu.CompilerParams(
            collective_id=1, has_side_effects=True, vmem_limit_bytes=63 << 20
        ),
        name="layer",
    )(*arrays)


def shards(
    attn_query, attn_key, attn_value, moe_input, cotangent,
    routes, route_weight, w_gate, w_up, w_down,
):
    expert_ids = jnp.arange(8, dtype=jnp.int32)
    hits = routes.T[:, None, :] == expert_ids[None, :, None]
    table = jnp.sum(
        jnp.where(hits, route_weight.astype(jnp.float32).T[:, None, :], 0.0), axis=0
    )
    results = layer(
        moe_input, cotangent, table, attn_query, attn_key, attn_value, w_gate, w_up, w_down
    )
    return tuple(results[:7])


def solution(mesh):
    tokens = P(("dp", "expert", "seq"), None)
    weights = P("expert", None, None)
    return jax.shard_map(
        shards,
        mesh=mesh,
        in_specs=(tokens,) * 7 + (weights,) * 3,
        out_specs=(tokens,) * 4 + (weights,) * 3,
        check_vma=False,
    )
```

```python
import functools
import math

import jax
import jax.numpy as jnp
from jax import lax
from jax.experimental import pallas as pl
from jax.experimental.pallas import tpu as pltpu
from jax.sharding import PartitionSpec as P

TOP = 2

HD = 128
NT = (((1,), (1,)), ((), ()))


def dot(a, b):
    return jnp.dot(a, b, preferred_element_type=jnp.float32)


def dot_nt(a, b):
    return lax.dot_general(a, b, NT, preferred_element_type=jnp.float32)


MESH = pl.DeviceIdType.MESH
ANY = pl.BlockSpec(memory_space=pl.ANY)


def enter(targets):
    barrier = pltpu.get_barrier_semaphore()
    for target in targets:
        pl.semaphore_signal(barrier, inc=1, device_id=target, device_id_type=MESH)
    pl.semaphore_wait(barrier, len(targets))


def remote(src, dst, send_sem, recv_sem, target):
    return pltpu.make_async_remote_copy(
        src_ref=src,
        dst_ref=dst,
        send_sem=send_sem,
        recv_sem=recv_sem,
        device_id=target,
        device_id_type=MESH,
    )


def strip(index, size):
    return pl.ds(pl.multiple_of(index * size, size), size)


def start_to_heads(srcs, dsts, send_sem, recv_sem, local_sem):
    me = lax.axis_index("seq")
    copies = []
    for a, (src, dst) in enumerate(zip(srcs, dsts)):
        for d in range(1, 8):
            to = lax.rem(me + d, 8)
            copies.append(
                remote(
                    src.at[:, strip(to, 256)],
                    dst.at[strip(me, 256), :],
                    send_sem.at[a, d],
                    recv_sem.at[a, d],
                    {"seq": to},
                )
            )
            copies[-1].start()
        copies.append(
            pltpu.make_async_copy(
                src.at[:, strip(me, 256)], dst.at[strip(me, 256), :], local_sem.at[a]
            )
        )
        copies[-1].start()
    return copies


def seq_peers():
    me = lax.axis_index("seq")
    return [{"seq": lax.rem(me + d, 8)} for d in range(1, 8)]


def sibling(index):
    return index + 1 - 2 * lax.rem(index, 2)


def dot_tn(a, b):
    return lax.dot_general(a, b, (((0,), (0,)), ((), ())), preferred_element_type=jnp.float32)


def flip(index):
    return index + 1 - 2 * lax.rem(index, 2)


def add_rows(out, base, terms, rows, step=16):
    @pl.loop(0, rows, step=step)
    def _(at):
        total = None
        for ref, start in terms:
            value = ref[pl.ds(pl.multiple_of(start + at, step), step), :].astype(jnp.float32)
            total = value if total is None else total + value
        out[pl.ds(pl.multiple_of(base + at, step), step), :] = total.astype(jnp.bfloat16)


def layer_kernel(
    x_ref, c_ref, t_ref, q_ref, k_ref, v_ref, wg_ref, wu_ref, wd_ref,
    gh_out, dq_out, dk_out, dv_out, gate_out, up_out, down_out, head_q, head_k, head_v,
    tokens, all_t, wg, wu, wd, own_weight, own_rank, pick, pick_weight, pick_t,
    rows_in, values, scaled, inner, grad_gate, grad_up, hidden, stage, joined,
    sib, z1, z2, wrecv, shard, do, ot, inv, dot_t, dqt,
    send_sem, recv_sem, load_sem, t_send, t_recv, seq_send, seq_recv, seq_local,
    sib_send, sib_recv, z_send, z_recv, rs_send, rs_recv, ag_send, ag_recv,
    gh_send, gh_recv, gh_local, out_send, out_recv, out_local, store_sem, shard_sem,
):
    me = lax.axis_index("expert")
    seq = lax.axis_index("seq")
    dp = lax.axis_index("dp")
    z, core = lax.div(me, 2), lax.rem(me, 2)
    far, near = lax.div(seq, 4), lax.rem(seq, 4)
    right, left, across = [lax.rem(me + d, 8) for d in (2, 6, 4)]
    pair = sibling(me)
    z_a, z_b = flip(z), 3 - z
    to_pair = {"expert": pair}
    to_a = {"expert": z_a * 2 + core}
    to_b = {"expert": z_b * 2 + core}
    hops = {
        "xa": ({"seq": far * 4 + flip(near)}, lax.rem(lax.div(near, 2) + lax.rem(near, 2), 2)),
        "xb": ({"seq": far * 4 + 3 - near}, lax.div(near, 2)),
        "ya": ({"dp": 1 - dp}, lax.rem(far + dp, 2)),
        "yb": ({"dp": 1 - dp, "seq": (1 - far) * 4 + near}, far),
    }
    orders = [
        ("xa", "xb", "ya", "yb"), ("xb", "xa", "yb", "ya"),
        ("ya", "yb", "xa", "xb"), ("yb", "ya", "xb", "xa"),
    ]
    enter(
        [{"expert": lax.rem(me + d, 8)} for d in range(1, 8)]
        + seq_peers()
        + [hops["ya"][0], hops["yb"][0]]
    )
    srcs = (x_ref, c_ref)
    sends = []

    def piece(a, half, owner, mine, target, send_at, recv_at):
        rows = pl.ds(half * 128, 128)
        dst = tokens.at[a * 8 + owner, rows, :]
        src = srcs[a].at[rows, :] if mine else dst
        return remote(src, dst, send_sem.at[send_at], recv_sem.at[recv_at], {"expert": target})

    def recv_index(kind, a, half):
        return kind * 4 + a * 2 + half

    def send(a, half, owner, mine, target, kind):
        copy = piece(a, half, owner, mine, target, len(sends), recv_index(kind, a, half))
        copy.start()
        sends.append(copy)

    def arrived(a, half, owner, kind):
        piece(a, half, owner, False, me, 0, recv_index(kind, a, half)).wait_recv()

    small = []
    for d in range(1, 8):
        to = lax.rem(me + d, 8)
        copy = remote(t_ref, all_t.at[me], t_send.at[d], t_recv.at[d], {"expert": to})
        copy.start()
        small.append(copy)
    for a in (0, 1):
        for half in (0, 1):
            send(a, half, me, True, pair, 3)
        for half in (0, 1):
            send(a, half, me, True, right, 0)
            send(a, 1 - half, me, True, left, 1)
    loads = [
        pltpu.make_async_copy(src, dst, load_sem.at[n])
        for n, (src, dst) in enumerate((
            (t_ref, all_t.at[me]), (x_ref, tokens.at[me]), (wg_ref.at[0], wg), (wu_ref.at[0], wu),
            (c_ref, tokens.at[8 + me]), (wd_ref.at[0], wd),
        ))
    ]
    for copy in loads:
        copy.start()
    heads = start_to_heads(
        (q_ref, k_ref, v_ref), (head_q, head_k, head_v), seq_send, seq_recv, seq_local
    )

    loads[0].wait()
    for copy in small:
        copy.wait_recv()
    for b in range(8):
        own_weight[pl.ds(b, 1), :] = all_t[b, pl.ds(me, 1), :]
    before = lax.broadcasted_iota(jnp.int32, (256, 256), 0)
    after = lax.broadcasted_iota(jnp.int32, (256, 256), 1)
    upto = jnp.where(before <= after, 1.0, 0.0).astype(jnp.bfloat16)
    taken = jnp.where(own_weight[...] > 0.0, 1.0, 0.0).astype(jnp.bfloat16)
    own_rank[...] = dot(taken, upto) - 1.0

    def fill_picks(b, carry):
        weight = own_weight[pl.ds(b, 1), :]
        rank = own_rank[pl.ds(b, 1), :]
        slot = lax.broadcasted_iota(jnp.int32, (128, 256), 0).astype(jnp.float32)
        hit = (slot == rank) & (weight > 0.0)
        chosen = jnp.where(hit, 1.0, 0.0)
        pick[b] = chosen.astype(jnp.bfloat16)
        pick_weight[b] = jnp.where(hit, jnp.broadcast_to(weight, hit.shape), 0.0).astype(jnp.bfloat16)
        pick_t[b] = chosen.T.astype(jnp.bfloat16)
        return carry

    lax.fori_loop(0, 8, fill_picks, 0)

    sizes, lands = (8, 4, 2, 1), (0, 8, 12, 14)
    send_at, keep_at = [], []
    for p in range(4):
        base, sent, kept = 0, [], []
        for i in range(4):
            bit = hops[orders[p][i]][1]
            sent.append(base + (1 - bit) * sizes[i])
            base = base + bit * sizes[i]
            kept.append(base)
        send_at.append(sent)
        keep_at.append(kept)

    def rs_copy(p, i):
        return remote(
            joined.at[p, pl.ds(send_at[p][i], sizes[i])],
            wrecv.at[p, pl.ds(lands[i], sizes[i])],
            rs_send.at[p, i], rs_recv.at[p, i], hops[orders[p][i]][0],
        )

    def rs_step(i):
        for p in range(4):
            rs_copy(p, i - 1).wait_recv()
            at = keep_at[p][i - 1]
            if i < 4:
                def add(r, carry):
                    total = joined[p, at + r].astype(jnp.float32) + wrecv[p, lands[i - 1] + r].astype(jnp.float32)
                    joined[p, at + r] = total.astype(jnp.bfloat16)
                    return carry

                lax.fori_loop(0, sizes[i - 1], add, 0)
                rs_copy(p, i).start()
            else:
                total = joined[p, at].astype(jnp.float32) + wrecv[p, 14].astype(jnp.float32)
                shard[p] = (total * (1.0 / 16.0)).astype(jnp.bfloat16)

    def final_rows(p, i, m):
        start, rows = keep_at[p][3 - i] * 32, sizes[3 - i] * 32
        if m < 2:
            return (gate_out, up_out)[m].at[0, pl.ds(pl.multiple_of(p * 512 + start, 32), rows), :]
        return down_out.at[0, pl.ds(pl.multiple_of(start, 32), rows), pl.ds(p * 512, 512)]

    def ag_copy(p, i, m):
        dst = final_rows(p, i, m)
        src = shard.at[p, pl.ds(m * 32, 32), :] if i == 0 else dst
        return remote(src, dst, ag_send.at[p, i, m], ag_recv.at[p, i, m], hops[orders[p][3 - i]][0])

    def store_shard(p, m):
        return pltpu.make_async_copy(
            shard.at[p, pl.ds(m * 32, 32), :], final_rows(p, 0, m), shard_sem.at[p, m]
        )

    def ag_step(i):
        for p in range(4):
            for m in range(3):
                if i == 0:
                    store_shard(p, m).start()
                if i == 1:
                    store_shard(p, m).wait()
                if i > 0:
                    ag_copy(p, i - 1, m).wait_recv()
            for m in range(3):
                if i < 4:
                    ag_copy(p, i, m).start()

    def gather_rows(chooser, first, base, out):
        for i in range(2):
            block = base + i

            @pl.loop(0, 2048, step=512)
            def _(at):
                cols = pl.ds(pl.multiple_of(at, 512), 512)
                out[pl.ds(i * 128, 128), cols] = dot(
                    chooser[block], tokens[first + block, :, cols]
                ).astype(jnp.bfloat16)

    def first_half(n, chip):
        gather_rows(pick, 0, chip * 2, rows_in.at[n])
        values[n // 2 % 2 if n < 3 else 0, 0] = dot(rows_in[n], wg[...])
        values[n // 2 % 2 if n < 3 else 0, 1] = dot(rows_in[n], wu[...])

    def sib_copy(n):
        return remote(stage.at[n % 2], sib.at[n], sib_send.at[n], sib_recv.at[n], to_pair)

    def scatter_rows(chip, which, out):
        @pl.loop(0, 2048, step=512)
        def _(at):
            cols = pl.ds(pl.multiple_of(at, 512), 512)
            out[:, cols] = dot(
                pick_t[chip * 2 + which], hidden[pl.ds(pl.multiple_of(which * 128, 128), 128), cols]
            ).astype(jnp.bfloat16)

    def weight_part(n, j):
        cols = strip(j, 512)
        for m, (a, b) in enumerate((
            (rows_in.at[n, :, cols], grad_gate), (rows_in.at[n, :, cols], grad_up), (inner, scaled.at[:, cols]),
        )):
            rows = pl.ds(m * 32, 32)
            value = dot_tn(a[...], b[...]).reshape(16, 32, 512)
            if n > 0:
                value += joined[j, :, rows, :].astype(jnp.float32)
            joined[j, :, rows, :] = value.astype(jnp.bfloat16)

    def second_half(n, chip):
        gather_rows(pick_weight, 8, chip * 2, scaled)
        grad_inner = dot_nt(scaled[...], wd[...])
        slot = 1 if n == 2 else 0
        gate, up = values[slot, 0], values[slot, 1]
        sig = jax.nn.sigmoid(gate)
        active = gate * sig
        inner[...] = (active * up).astype(jnp.bfloat16)
        grad_gate[...] = (grad_inner * up * sig * (1.0 + gate * (1.0 - sig))).astype(jnp.bfloat16)
        grad_up[...] = (grad_inner * active).astype(jnp.bfloat16)

        if n == 3:
            for j in range(4):
                weight_part(n, j)
                rs_copy(j, 0).start()

        @pl.loop(0, 2048, step=512)
        def _(at):
            cols = pl.ds(pl.multiple_of(at, 512), 512)
            hidden[:, cols] = (
                dot_nt(grad_gate[...], wg[cols, :]) + dot_nt(grad_up[...], wu[cols, :])
            ).astype(jnp.bfloat16)

        if n >= 2:
            sib_copy(n - 2).wait_send()
        scatter_rows(chip, 1 - core, stage.at[n % 2])
        sib_copy(n).start()
        if n < 3:
            @pl.loop(0, 4)
            def _(j):
                weight_part(n, j)

        scatter_rows(chip, core, rows_in.at[n])

    def pair_arrived(a, kind, owner):
        for half in (0, 1):
            arrived(a, half, sibling(owner), kind)

    def relay(a):
        arrived(a, 0, left, 0)
        send(a, 0, left, False, right, 2)
        send(a, 0, left, False, pair, 4)
        arrived(a, 1, right, 1)
        send(a, 1, right, False, left, 2)
        send(a, 1, right, False, pair, 5)
        arrived(a, 1, left, 0)
        send(a, 1, left, False, pair, 4)
        arrived(a, 0, right, 1)
        send(a, 0, right, False, pair, 5)

    def relay_last(a):
        for half in (0, 1):
            arrived(a, half, across, 2)
            send(a, half, across, False, pair, 6)

    def z_copy(n):
        first, second = pl.ds(0, 128), pl.ds(128, 128)
        src, dst, target = (
            (rows_in.at[3, first, :], z1.at[0, 0], to_a),
            (rows_in.at[3, second, :], z1.at[1, 0], to_b),
            (rows_in.at[1, first, :], z1.at[0, 1], to_a),
            (rows_in.at[2, second, :], z1.at[1, 1], to_b),
            (rows_in.at[2, first, :], z2.at[0], to_b),
            (rows_in.at[1, second, :], z2.at[1], to_a),
        )[n]
        return remote(src, dst, z_send.at[n], z_recv.at[n], target)

    def pair_sum(n):
        sib_copy(n).wait_recv()
        add_rows(rows_in.at[n], 0, [(rows_in.at[n], 0), (sib.at[n], 0)], 256)

    owner_a, owner_b = z_a * 2 + core, z_b * 2 + core
    kind_a = 5 - lax.rem(z, 2)
    kind_b = 9 - kind_a
    loads[1].wait()
    pair_arrived(0, 3, me)
    loads[2].wait()
    loads[3].wait()
    first_half(0, z)
    loads[4].wait()
    pair_arrived(1, 3, me)
    loads[5].wait()
    second_half(0, z)
    relay(0)
    pair_arrived(0, kind_a, owner_a)
    first_half(1, z_a)
    pair_arrived(0, kind_b, owner_b)
    first_half(2, z_b)
    relay(1)
    pair_arrived(1, kind_a, owner_a)
    second_half(1, z_a)
    relay_last(0)
    pair_arrived(1, kind_b, owner_b)
    second_half(2, z_b)
    pair_arrived(0, 6, across)
    first_half(3, lax.div(across, 2))
    pair_sum(1)
    pair_sum(2)
    relay_last(1)
    z_copy(2).start()
    z_copy(3).start()
    pair_arrived(1, 6, across)
    second_half(3, lax.div(across, 2))

    for copy in heads:
        copy.wait()
    head_loads = []
    for n, (src, dst, at) in enumerate(((head_q, wg, 0), (head_k, wg, 256), (head_v, wu, 0))):
        head_loads.append(
            pltpu.make_async_copy(src, dst.at[:, pl.ds(at, 256)], load_sem.at[6 + n])
        )
    cot_load = pltpu.make_async_copy(c_ref, scaled, load_sem.at[9])
    for copy in head_loads + [cot_load]:
        copy.start()
    pair_sum(3)
    z_copy(0).start()
    z_copy(1).start()
    for copy in sends + small:
        copy.wait_send()
    for copy in head_loads:
        copy.wait()

    def lanes(h):
        return pl.ds(pl.multiple_of(h * HD, HD), HD)

    def key_lanes(h):
        return pl.ds(pl.multiple_of(256 + h * HD, HD), HD)

    for h in range(2):
        wd[lanes(h), :] = wu[:, lanes(h)].T

    def forward_block(index, carry):
        h, at = lax.div(index, 8), lax.rem(index, 8)
        cols = strip(at, 256)
        to_exp2 = (HD ** -0.5) * math.log2(math.e)
        query = wg[cols, lanes(h)]
        top = None
        for i in range(8):
            score = dot_nt(wg[pl.ds(i * 256, 256), key_lanes(h)], query)
            values[i // 4, i // 2 % 2, :, pl.ds(i % 2 * 256, 256)] = score
            peak = jnp.max(score, axis=0, keepdims=True)
            top = peak if top is None else jnp.maximum(top, peak)
        total = jnp.zeros((1, 256), jnp.float32)
        attended = jnp.zeros((HD, 256), jnp.float32)
        for i in range(8):
            score = values[i // 4, i // 2 % 2, :, pl.ds(i % 2 * 256, 256)]
            expo = jnp.exp2((score - top) * to_exp2)
            total += jnp.sum(expo, axis=0, keepdims=True)
            expo = expo.astype(jnp.bfloat16)
            tokens[h * 8 + i, :, cols] = expo
            attended += dot(wd[lanes(h), pl.ds(i * 256, 256)], expo)
        scale = 1.0 / total
        ot[h, :, cols] = attended
        inv[h, :, cols] = scale
        wd[key_lanes(h), cols] = (query.astype(jnp.float32).T * scale).astype(jnp.bfloat16)
        return carry

    def forward(first, last):
        lax.fori_loop(first, last, forward_block, 0)

    forward(0, 6)
    rs_step(1)
    z_copy(0).wait_recv()
    add_rows(rows_in.at[2], 0, [(rows_in.at[2], 0), (z1.at[0, 0], 0)], 128)
    z_copy(4).start()
    z_copy(1).wait_recv()
    add_rows(rows_in.at[1], 128, [(rows_in.at[1], 128), (z1.at[1, 0], 0)], 128)
    z_copy(5).start()
    forward(6, 10)
    rs_step(2)
    forward(10, 13)
    cot_load.wait()
    sib_copy(0).wait_recv()
    sib_copy(2).wait_send()
    gh = stage.at[0]
    for p in range(2):
        z_copy(2 + p).wait_recv()
        z_copy(4 + p).wait_recv()
        add_rows(
            gh, 128 * p,
            [
                (scaled, 128 * p), (rows_in.at[0], 128 * p), (sib.at[0], 128 * p),
                (z1.at[p, 1], 0), (z2.at[p], 0),
            ],
            128,
        )
    gh_copies = []
    for d in range(1, 8):
        to = lax.rem(seq + d, 8)
        copy = remote(
            gh.at[:, strip(to, 256)], do.at[strip(seq, 256), :], gh_send.at[d], gh_recv.at[d], {"seq": to}
        )
        copy.start()
        gh_copies.append(copy)
    gh_own = pltpu.make_async_copy(gh.at[:, strip(seq, 256)], do.at[strip(seq, 256), :], gh_local)
    gh_own.start()
    gh_store = pltpu.make_async_copy(gh, gh_out, store_sem)
    gh_store.start()
    rs_step(3)
    forward(13, 16)
    rs_step(4)
    ag_step(0)
    for h in range(2):
        wd[lanes(h), :] = wg[:, key_lanes(h)].T
    ag_step(1)
    for copy in gh_copies:
        copy.wait_recv()
    gh_own.wait()
    ag_step(2)

    scale = HD ** -0.5
    outs = (dq_out, dk_out, dv_out)

    def back(n, h, rows):
        return (wg, wg, wu)[n].at[rows, key_lanes(h) if n == 1 else lanes(h)]

    def out_copy(h, n, d):
        to = lax.rem(seq + d, 8)
        return remote(
            back(n, h, strip(to, 256)), outs[n].at[:, lanes(seq * 2 + h)],
            out_send.at[h, n, d], out_recv.at[h, n, d], {"seq": to},
        )

    def out_own(h, n):
        return pltpu.make_async_copy(
            back(n, h, strip(seq, 256)), outs[n].at[:, lanes(seq * 2 + h)], out_local.at[h, n]
        )

    for h in range(2):
        head = pl.ds(h * HD, HD)
        norm = inv[h]
        grad_t = do[:, head].astype(jnp.float32).T
        delta = jnp.sum(grad_t * ot[h], axis=0, keepdims=True) * norm
        dot_t[...] = (grad_t * norm).astype(jnp.bfloat16)
        dqt[...] = jnp.zeros_like(dqt)

        def chunk(d, carry):
            at = lax.rem(seq + d, 8)
            rows = strip(at, 256)
            expo = tokens[h * 8 + at]
            grad_probs = dot_nt(wu[rows, head], do[:, head])
            hidden[...] = (expo.astype(jnp.float32) * (grad_probs - delta)).astype(jnp.bfloat16)
            wu[rows, head] = dot_nt(expo, dot_t[...]).astype(jnp.bfloat16)
            wg[rows, key_lanes(h)] = (dot_nt(hidden[...], wd[key_lanes(h), :]) * scale).astype(jnp.bfloat16)
            dqt[...] += dot(wd[lanes(h), rows], hidden[...])

            @pl.when(d > 0)
            def _():
                out_copy(h, 1, d).start()
                out_copy(h, 2, d).start()

            return carry

        lax.fori_loop(0, 4, chunk, 0)
        if h == 0:
            ag_step(3)
        lax.fori_loop(4, 8, chunk, 0)
        wg[:, head] = (dqt[...] * (norm * scale)).T.astype(jnp.bfloat16)
        for d in range(1, 8):
            out_copy(h, 0, d).start()
        for n in range(3):
            out_own(h, n).start()
    ag_step(4)

    sib_copy(3).wait_send()
    for copy in gh_copies:
        copy.wait_send()
    for n in range(6):
        z_copy(n).wait_send()
    for p in range(4):
        for i in range(4):
            rs_copy(p, i).wait_send()
            for m in range(3):
                ag_copy(p, i, m).wait_send()
    gh_store.wait()
    for h in range(2):
        for n in range(3):
            out_own(h, n).wait()
            for d in range(1, 8):
                out_copy(h, n, d).wait()


def layer(*arrays):
    dma = pltpu.SemaphoreType.DMA
    bf16, f32 = jnp.bfloat16, jnp.float32
    shapes = [(256, 2048)] * 4 + [(1, 2048, 512)] * 2 + [(1, 512, 2048)] + [(2048, 256)] * 3
    vmem = [
        ((16, 256, 2048), bf16), ((8, 8, 256), f32),
        ((2048, 512), bf16), ((2048, 512), bf16), ((512, 2048), bf16),
        ((8, 256), f32), ((8, 256), f32),
        ((8, 128, 256), bf16), ((8, 128, 256), bf16), ((8, 256, 128), bf16),
        ((4, 256, 2048), bf16), ((2, 2, 256, 512), f32),
        ((256, 2048), bf16), ((256, 512), bf16), ((256, 512), bf16), ((256, 512), bf16),
        ((256, 2048), bf16), ((2, 256, 2048), bf16), ((4, 16, 96, 512), bf16),
        ((4, 256, 2048), bf16), ((2, 2, 128, 2048), bf16), ((2, 128, 2048), bf16),
        ((4, 15, 96, 512), bf16), ((4, 96, 512), bf16), ((2048, 256), bf16),
        ((2, HD, 2048), f32), ((2, 1, 2048), f32), ((HD, 2048), bf16), ((HD, 2048), f32),
    ]
    sems = [
        (28,), (28,), (10,), (8,), (8,), (3, 8), (3, 8), (3,),
        (4,), (4,), (6,), (6,), (4, 4), (4, 4), (4, 4, 3), (4, 4, 3),
        (8,), (8,), (), (2, 3, 8), (2, 3, 8), (2, 3), (), (4, 3),
    ]
    return pl.pallas_call(
        layer_kernel,
        out_shape=[jax.ShapeDtypeStruct(shape, bf16) for shape in shapes],
        in_specs=[ANY] * len(arrays),
        out_specs=[ANY] * len(shapes),
        scratch_shapes=[pltpu.VMEM(*kind) for kind in vmem] + [dma(s) if s else dma for s in sems],
        compiler_params=pltpu.CompilerParams(
            collective_id=1, has_side_effects=True, vmem_limit_bytes=63 << 20
        ),
        name="layer",
    )(*arrays)


def finish_kernel(*refs):
    count = (len(refs) - 2) // 3
    srcs, dsts, bufs = refs[:count], refs[count : 2 * count], refs[2 * count : 3 * count]
    read_sem, write_sem = refs[3 * count :]
    reads = [pltpu.make_async_copy(src, buf, read_sem.at[n]) for n, (src, buf) in enumerate(zip(srcs, bufs))]
    writes = [pltpu.make_async_copy(buf, dst, write_sem.at[n]) for n, (buf, dst) in enumerate(zip(bufs, dsts))]
    for read in reads:
        read.start()
    for read, write in zip(reads, writes):
        read.wait()
        write.start()
    for write in writes:
        write.wait()


def finish(arrays):
    count = len(arrays)
    return pl.pallas_call(
        finish_kernel,
        out_shape=[jax.ShapeDtypeStruct(a.shape, a.dtype) for a in arrays],
        in_specs=[ANY] * count,
        out_specs=[ANY] * count,
        scratch_shapes=[pltpu.VMEM(a.shape, a.dtype) for a in arrays]
        + [pltpu.SemaphoreType.DMA((count,)), pltpu.SemaphoreType.DMA((count,))],
        compiler_params=pltpu.CompilerParams(vmem_limit_bytes=62 << 20),
        name="finish",
    )(*arrays)


def shards(
    attn_query, attn_key, attn_value, moe_input, cotangent,
    routes, route_weight, w_gate, w_up, w_down,
):
    expert_ids = jnp.arange(8, dtype=jnp.int32)
    hits = routes.T[:, None, :] == expert_ids[None, :, None]
    table = jnp.sum(
        jnp.where(hits, route_weight.astype(jnp.float32).T[:, None, :], 0.0), axis=0
    )
    results = layer(
        moe_input, cotangent, table, attn_query, attn_key, attn_value, w_gate, w_up, w_down
    )
    return tuple(finish(results[:7]))


def solution(mesh):
    tokens = P(("dp", "expert", "seq"), None)
    weights = P("expert", None, None)
    return jax.shard_map(
        shards,
        mesh=mesh,
        in_specs=(tokens,) * 7 + (weights,) * 3,
        out_specs=(tokens,) * 4 + (weights,) * 3,
        check_vma=False,
    )
```

```python
import functools
import math

import jax
import jax.numpy as jnp
from jax import lax
from jax.experimental import pallas as pl
from jax.experimental.pallas import tpu as pltpu
from jax.sharding import PartitionSpec as P

TOP = 2

HD = 128
NT = (((1,), (1,)), ((), ()))


def dot(a, b):
    return jnp.dot(a, b, preferred_element_type=jnp.float32)


def dot_nt(a, b):
    return lax.dot_general(a, b, NT, preferred_element_type=jnp.float32)


MESH = pl.DeviceIdType.MESH
ANY = pl.BlockSpec(memory_space=pl.ANY)


def enter(targets):
    barrier = pltpu.get_barrier_semaphore()
    for target in targets:
        pl.semaphore_signal(barrier, inc=1, device_id=target, device_id_type=MESH)
    pl.semaphore_wait(barrier, len(targets))


def remote(src, dst, send_sem, recv_sem, target):
    return pltpu.make_async_remote_copy(
        src_ref=src,
        dst_ref=dst,
        send_sem=send_sem,
        recv_sem=recv_sem,
        device_id=target,
        device_id_type=MESH,
    )


def strip(index, size):
    return pl.ds(pl.multiple_of(index * size, size), size)


def start_to_heads(srcs, dsts, send_sem, recv_sem, local_sem):
    me = lax.axis_index("seq")
    copies = []
    for a, (src, dst) in enumerate(zip(srcs, dsts)):
        for d in range(1, 8):
            to = lax.rem(me + d, 8)
            copies.append(
                remote(
                    src.at[:, strip(to, 256)],
                    dst.at[strip(me, 256), :],
                    send_sem.at[a, d],
                    recv_sem.at[a, d],
                    {"seq": to},
                )
            )
            copies[-1].start()
        copies.append(
            pltpu.make_async_copy(
                src.at[:, strip(me, 256)], dst.at[strip(me, 256), :], local_sem.at[a]
            )
        )
        copies[-1].start()
    return copies


def seq_peers():
    me = lax.axis_index("seq")
    return [{"seq": lax.rem(me + d, 8)} for d in range(1, 8)]


def sibling(index):
    return index + 1 - 2 * lax.rem(index, 2)


def dot_tn(a, b):
    return lax.dot_general(a, b, (((0,), (0,)), ((), ())), preferred_element_type=jnp.float32)


def flip(index):
    return index + 1 - 2 * lax.rem(index, 2)


def add_rows(out, base, terms, rows, step=16):
    @pl.loop(0, rows, step=step)
    def _(at):
        total = None
        for ref, start in terms:
            value = ref[pl.ds(pl.multiple_of(start + at, step), step), :].astype(jnp.float32)
            total = value if total is None else total + value
        out[pl.ds(pl.multiple_of(base + at, step), step), :] = total.astype(jnp.bfloat16)


def layer_kernel(
    x_ref, c_ref, t_ref, q_ref, k_ref, v_ref, wg_ref, wu_ref, wd_ref,
    gh_out, dq_out, dk_out, dv_out, gate_out, up_out, down_out, head_q, head_k, head_v,
    tokens, all_t, wg, wu, wd, own_weight, own_rank, pick, pick_weight, pick_t,
    rows_in, values, scaled, inner, grad_gate, grad_up, hidden, stage, joined,
    sib, z1, z2, wrecv, shard, do, ot, inv, dot_t, dqt,
    send_sem, recv_sem, load_sem, t_send, t_recv, seq_send, seq_recv, seq_local,
    sib_send, sib_recv, z_send, z_recv, rs_send, rs_recv, ag_send, ag_recv,
    gh_send, gh_recv, gh_local, out_send, out_recv, out_local, store_sem, shard_sem,
):
    me = lax.axis_index("expert")
    seq = lax.axis_index("seq")
    dp = lax.axis_index("dp")
    z, core = lax.div(me, 2), lax.rem(me, 2)
    far, near = lax.div(seq, 4), lax.rem(seq, 4)
    right, left, across = [lax.rem(me + d, 8) for d in (2, 6, 4)]
    pair = sibling(me)
    z_a, z_b = flip(z), 3 - z
    to_pair = {"expert": pair}
    to_a = {"expert": z_a * 2 + core}
    to_b = {"expert": z_b * 2 + core}
    hops = {
        "xa": ({"seq": far * 4 + flip(near)}, lax.rem(lax.div(near, 2) + lax.rem(near, 2), 2)),
        "xb": ({"seq": far * 4 + 3 - near}, lax.div(near, 2)),
        "ya": ({"dp": 1 - dp}, lax.rem(far + dp, 2)),
        "yb": ({"dp": 1 - dp, "seq": (1 - far) * 4 + near}, far),
    }
    orders = [
        ("xa", "xb", "ya", "yb"), ("xb", "xa", "yb", "ya"),
        ("ya", "yb", "xa", "xb"), ("yb", "ya", "xb", "xa"),
    ]
    enter(
        [{"expert": lax.rem(me + d, 8)} for d in range(1, 8)]
        + seq_peers()
        + [hops["ya"][0], hops["yb"][0]]
    )
    srcs = (x_ref, c_ref)
    sends = []

    def piece(a, half, owner, mine, target, send_at, recv_at):
        rows = pl.ds(half * 128, 128)
        dst = tokens.at[a * 8 + owner, rows, :]
        src = srcs[a].at[rows, :] if mine else dst
        return remote(src, dst, send_sem.at[send_at], recv_sem.at[recv_at], {"expert": target})

    def recv_index(kind, a, half):
        return kind * 4 + a * 2 + half

    def send(a, half, owner, mine, target, kind):
        copy = piece(a, half, owner, mine, target, len(sends), recv_index(kind, a, half))
        copy.start()
        sends.append(copy)

    def arrived(a, half, owner, kind):
        piece(a, half, owner, False, me, 0, recv_index(kind, a, half)).wait_recv()

    small = []
    for d in range(1, 8):
        to = lax.rem(me + d, 8)
        copy = remote(t_ref, all_t.at[me], t_send.at[d], t_recv.at[d], {"expert": to})
        copy.start()
        small.append(copy)
    for a in (0, 1):
        for half in (0, 1):
            send(a, half, me, True, pair, 3)
        for half in (0, 1):
            send(a, half, me, True, right, 0)
            send(a, 1 - half, me, True, left, 1)
    loads = [
        pltpu.make_async_copy(src, dst, load_sem.at[n])
        for n, (src, dst) in enumerate((
            (t_ref, all_t.at[me]), (x_ref, tokens.at[me]), (wg_ref.at[0], wg), (wu_ref.at[0], wu),
            (c_ref, tokens.at[8 + me]), (wd_ref.at[0], wd),
        ))
    ]
    for copy in loads:
        copy.start()
    heads = start_to_heads(
        (q_ref, k_ref, v_ref), (head_q, head_k, head_v), seq_send, seq_recv, seq_local
    )

    loads[0].wait()
    for copy in small:
        copy.wait_recv()
    for b in range(8):
        own_weight[pl.ds(b, 1), :] = all_t[b, pl.ds(me, 1), :]
    before = lax.broadcasted_iota(jnp.int32, (256, 256), 0)
    after = lax.broadcasted_iota(jnp.int32, (256, 256), 1)
    upto = jnp.where(before <= after, 1.0, 0.0).astype(jnp.bfloat16)
    taken = jnp.where(own_weight[...] > 0.0, 1.0, 0.0).astype(jnp.bfloat16)
    own_rank[...] = dot(taken, upto) - 1.0

    def fill_picks(b, carry):
        weight = own_weight[pl.ds(b, 1), :]
        rank = own_rank[pl.ds(b, 1), :]
        slot = lax.broadcasted_iota(jnp.int32, (128, 256), 0).astype(jnp.float32)
        hit = (slot == rank) & (weight > 0.0)
        chosen = jnp.where(hit, 1.0, 0.0)
        pick[b] = chosen.astype(jnp.bfloat16)
        pick_weight[b] = jnp.where(hit, jnp.broadcast_to(weight, hit.shape), 0.0).astype(jnp.bfloat16)
        pick_t[b] = chosen.T.astype(jnp.bfloat16)
        return carry

    lax.fori_loop(0, 8, fill_picks, 0)

    sizes, lands = (8, 4, 2, 1), (0, 8, 12, 14)
    send_at, keep_at = [], []
    for p in range(4):
        base, sent, kept = 0, [], []
        for i in range(4):
            bit = hops[orders[p][i]][1]
            sent.append(base + (1 - bit) * sizes[i])
            base = base + bit * sizes[i]
            kept.append(base)
        send_at.append(sent)
        keep_at.append(kept)

    def rs_copy(p, i):
        return remote(
            joined.at[p, pl.ds(send_at[p][i], sizes[i])],
            wrecv.at[p, pl.ds(lands[i], sizes[i])],
            rs_send.at[p, i], rs_recv.at[p, i], hops[orders[p][i]][0],
        )

    def rs_step(i):
        for p in range(4):
            rs_copy(p, i - 1).wait_recv()
            at = keep_at[p][i - 1]
            if i < 4:
                def add(r, carry):
                    total = joined[p, at + r].astype(jnp.float32) + wrecv[p, lands[i - 1] + r].astype(jnp.float32)
                    joined[p, at + r] = total.astype(jnp.bfloat16)
                    return carry

                lax.fori_loop(0, sizes[i - 1], add, 0)
                rs_copy(p, i).start()
            else:
                total = joined[p, at].astype(jnp.float32) + wrecv[p, 14].astype(jnp.float32)
                shard[p] = (total * (1.0 / 16.0)).astype(jnp.bfloat16)

    def final_rows(p, i, m):
        start, rows = keep_at[p][3 - i] * 32, sizes[3 - i] * 32
        if m < 2:
            return (gate_out, up_out)[m].at[0, pl.ds(pl.multiple_of(p * 512 + start, 32), rows), :]
        return down_out.at[0, pl.ds(pl.multiple_of(start, 32), rows), pl.ds(p * 512, 512)]

    def ag_copy(p, i, m):
        dst = final_rows(p, i, m)
        src = shard.at[p, pl.ds(m * 32, 32), :] if i == 0 else dst
        return remote(src, dst, ag_send.at[p, i, m], ag_recv.at[p, i, m], hops[orders[p][3 - i]][0])

    def store_shard(p, m):
        return pltpu.make_async_copy(
            shard.at[p, pl.ds(m * 32, 32), :], final_rows(p, 0, m), shard_sem.at[p, m]
        )

    def ag_step(i):
        for p in range(4):
            for m in range(3):
                if i == 0:
                    store_shard(p, m).start()
                if i == 1:
                    store_shard(p, m).wait()
                if i > 0:
                    ag_copy(p, i - 1, m).wait_recv()
            for m in range(3):
                if i < 4:
                    ag_copy(p, i, m).start()

    def gather_rows(chooser, first, base, out):
        for i in range(2):
            block = base + i

            @pl.loop(0, 2048, step=512)
            def _(at):
                cols = pl.ds(pl.multiple_of(at, 512), 512)
                out[pl.ds(i * 128, 128), cols] = dot(
                    chooser[block], tokens[first + block, :, cols]
                ).astype(jnp.bfloat16)

    def first_half(n, chip):
        gather_rows(pick, 0, chip * 2, rows_in.at[n])
        values[n // 2 % 2 if n < 3 else 0, 0] = dot(rows_in[n], wg[...])
        values[n // 2 % 2 if n < 3 else 0, 1] = dot(rows_in[n], wu[...])

    def sib_copy(n):
        return remote(stage.at[n % 2], sib.at[n], sib_send.at[n], sib_recv.at[n], to_pair)

    def scatter_rows(chip, which, out):
        @pl.loop(0, 2048, step=512)
        def _(at):
            cols = pl.ds(pl.multiple_of(at, 512), 512)
            out[:, cols] = dot(
                pick_t[chip * 2 + which], hidden[pl.ds(pl.multiple_of(which * 128, 128), 128), cols]
            ).astype(jnp.bfloat16)

    def weight_part(n, j):
        cols = strip(j, 512)
        for m, (a, b) in enumerate((
            (rows_in.at[n, :, cols], grad_gate), (rows_in.at[n, :, cols], grad_up), (inner, scaled.at[:, cols]),
        )):
            rows = pl.ds(m * 32, 32)
            value = dot_tn(a[...], b[...]).reshape(16, 32, 512)
            if n > 0:
                value += joined[j, :, rows, :].astype(jnp.float32)
            joined[j, :, rows, :] = value.astype(jnp.bfloat16)

    def second_half(n, chip):
        gather_rows(pick_weight, 8, chip * 2, scaled)
        grad_inner = dot_nt(scaled[...], wd[...])
        slot = 1 if n == 2 else 0
        gate, up = values[slot, 0], values[slot, 1]
        sig = jax.nn.sigmoid(gate)
        active = gate * sig
        inner[...] = (active * up).astype(jnp.bfloat16)
        grad_gate[...] = (grad_inner * up * sig * (1.0 + gate * (1.0 - sig))).astype(jnp.bfloat16)
        grad_up[...] = (grad_inner * active).astype(jnp.bfloat16)

        if n == 3:
            for j in range(4):
                weight_part(n, j)
                rs_copy(j, 0).start()

        @pl.loop(0, 2048, step=512)
        def _(at):
            cols = pl.ds(pl.multiple_of(at, 512), 512)
            hidden[:, cols] = (
                dot_nt(grad_gate[...], wg[cols, :]) + dot_nt(grad_up[...], wu[cols, :])
            ).astype(jnp.bfloat16)

        if n >= 2:
            sib_copy(n - 2).wait_send()
        scatter_rows(chip, 1 - core, stage.at[n % 2])
        sib_copy(n).start()
        if n < 3:
            @pl.loop(0, 4)
            def _(j):
                weight_part(n, j)

        scatter_rows(chip, core, rows_in.at[n])

    def pair_arrived(a, kind, owner):
        for half in (0, 1):
            arrived(a, half, sibling(owner), kind)

    def relay(a):
        arrived(a, 0, left, 0)
        send(a, 0, left, False, right, 2)
        send(a, 0, left, False, pair, 4)
        arrived(a, 1, right, 1)
        send(a, 1, right, False, left, 2)
        send(a, 1, right, False, pair, 5)
        arrived(a, 1, left, 0)
        send(a, 1, left, False, pair, 4)
        arrived(a, 0, right, 1)
        send(a, 0, right, False, pair, 5)

    def relay_last(a):
        for half in (0, 1):
            arrived(a, half, across, 2)
            send(a, half, across, False, pair, 6)

    def z_copy(n):
        first, second = pl.ds(0, 128), pl.ds(128, 128)
        src, dst, target = (
            (rows_in.at[3, first, :], z1.at[0, 0], to_a),
            (rows_in.at[3, second, :], z1.at[1, 0], to_b),
            (rows_in.at[1, first, :], z1.at[0, 1], to_a),
            (rows_in.at[2, second, :], z1.at[1, 1], to_b),
            (rows_in.at[2, first, :], z2.at[0], to_b),
            (rows_in.at[1, second, :], z2.at[1], to_a),
        )[n]
        return remote(src, dst, z_send.at[n], z_recv.at[n], target)

    def pair_sum(n):
        sib_copy(n).wait_recv()
        add_rows(rows_in.at[n], 0, [(rows_in.at[n], 0), (sib.at[n], 0)], 256)

    owner_a, owner_b = z_a * 2 + core, z_b * 2 + core
    kind_a = 5 - lax.rem(z, 2)
    kind_b = 9 - kind_a
    loads[1].wait()
    pair_arrived(0, 3, me)
    loads[2].wait()
    loads[3].wait()
    first_half(0, z)
    loads[4].wait()
    pair_arrived(1, 3, me)
    loads[5].wait()
    second_half(0, z)
    relay(0)
    pair_arrived(0, kind_a, owner_a)
    first_half(1, z_a)
    pair_arrived(0, kind_b, owner_b)
    first_half(2, z_b)
    relay(1)
    pair_arrived(1, kind_a, owner_a)
    second_half(1, z_a)
    relay_last(0)
    pair_arrived(1, kind_b, owner_b)
    second_half(2, z_b)
    pair_arrived(0, 6, across)
    first_half(3, lax.div(across, 2))
    pair_sum(1)
    pair_sum(2)
    relay_last(1)
    z_copy(2).start()
    z_copy(3).start()
    pair_arrived(1, 6, across)
    second_half(3, lax.div(across, 2))

    for copy in heads:
        copy.wait()
    head_loads = []
    for n, (src, dst, at) in enumerate(((head_q, wg, 0), (head_k, wg, 256), (head_v, wu, 0))):
        head_loads.append(
            pltpu.make_async_copy(src, dst.at[:, pl.ds(at, 256)], load_sem.at[6 + n])
        )
    cot_load = pltpu.make_async_copy(c_ref, scaled, load_sem.at[9])
    for copy in head_loads + [cot_load]:
        copy.start()
    pair_sum(3)
    z_copy(0).start()
    z_copy(1).start()
    for copy in sends + small:
        copy.wait_send()
    for copy in head_loads:
        copy.wait()

    def lanes(h):
        return pl.ds(pl.multiple_of(h * HD, HD), HD)

    def key_lanes(h):
        return pl.ds(pl.multiple_of(256 + h * HD, HD), HD)

    for h in range(2):
        wd[lanes(h), :] = wu[:, lanes(h)].T

    def forward_block(index, carry):
        h, at = lax.div(index, 8), lax.rem(index, 8)
        cols = strip(at, 256)
        to_exp2 = (HD ** -0.5) * math.log2(math.e)
        query = wg[cols, lanes(h)]
        top = None
        for i in range(8):
            score = dot_nt(wg[pl.ds(i * 256, 256), key_lanes(h)], query)
            values[i // 4, i // 2 % 2, :, pl.ds(i % 2 * 256, 256)] = score
            peak = jnp.max(score, axis=0, keepdims=True)
            top = peak if top is None else jnp.maximum(top, peak)
        total = jnp.zeros((1, 256), jnp.float32)
        attended = jnp.zeros((HD, 256), jnp.float32)
        for i in range(8):
            score = values[i // 4, i // 2 % 2, :, pl.ds(i % 2 * 256, 256)]
            expo = jnp.exp2((score - top) * to_exp2)
            total += jnp.sum(expo, axis=0, keepdims=True)
            expo = expo.astype(jnp.bfloat16)
            tokens[h * 8 + i, :, cols] = expo
            attended += dot(wd[lanes(h), pl.ds(i * 256, 256)], expo)
        scale = 1.0 / total
        ot[h, :, cols] = attended
        inv[h, :, cols] = scale
        wd[key_lanes(h), cols] = (query.astype(jnp.float32).T * scale).astype(jnp.bfloat16)
        return carry

    def forward(first, last):
        lax.fori_loop(first, last, forward_block, 0)

    forward(0, 6)
    rs_step(1)
    z_copy(0).wait_recv()
    add_rows(rows_in.at[2], 0, [(rows_in.at[2], 0), (z1.at[0, 0], 0)], 128)
    z_copy(4).start()
    z_copy(1).wait_recv()
    add_rows(rows_in.at[1], 128, [(rows_in.at[1], 128), (z1.at[1, 0], 0)], 128)
    z_copy(5).start()
    forward(6, 10)
    rs_step(2)
    forward(10, 13)
    rs_step(3)
    rs_step(4)
    ag_step(0)
    cot_load.wait()
    sib_copy(0).wait_recv()
    sib_copy(2).wait_send()
    gh = stage.at[0]
    for p in range(2):
        z_copy(2 + p).wait_recv()
        z_copy(4 + p).wait_recv()
        add_rows(
            gh, 128 * p,
            [
                (scaled, 128 * p), (rows_in.at[0], 128 * p), (sib.at[0], 128 * p),
                (z1.at[p, 1], 0), (z2.at[p], 0),
            ],
            128,
        )
    gh_copies = []
    for d in range(1, 8):
        to = lax.rem(seq + d, 8)
        copy = remote(
            gh.at[:, strip(to, 256)], do.at[strip(seq, 256), :], gh_send.at[d], gh_recv.at[d], {"seq": to}
        )
        copy.start()
        gh_copies.append(copy)
    gh_own = pltpu.make_async_copy(gh.at[:, strip(seq, 256)], do.at[strip(seq, 256), :], gh_local)
    gh_own.start()
    gh_store = pltpu.make_async_copy(gh, gh_out, store_sem)
    gh_store.start()
    ag_step(1)
    forward(13, 16)
    ag_step(2)
    for h in range(2):
        wd[lanes(h), :] = wg[:, key_lanes(h)].T
    for copy in gh_copies:
        copy.wait_recv()
    gh_own.wait()
    ag_step(3)

    scale = HD ** -0.5
    outs = (dq_out, dk_out, dv_out)

    def back(n, h, rows):
        return (wg, wg, wu)[n].at[rows, key_lanes(h) if n == 1 else lanes(h)]

    def out_copy(h, n, d):
        to = lax.rem(seq + d, 8)
        return remote(
            back(n, h, strip(to, 256)), outs[n].at[:, lanes(seq * 2 + h)],
            out_send.at[h, n, d], out_recv.at[h, n, d], {"seq": to},
        )

    def out_own(h, n):
        return pltpu.make_async_copy(
            back(n, h, strip(seq, 256)), outs[n].at[:, lanes(seq * 2 + h)], out_local.at[h, n]
        )

    for h in range(2):
        head = pl.ds(h * HD, HD)
        norm = inv[h]
        grad_t = do[:, head].astype(jnp.float32).T
        delta = jnp.sum(grad_t * ot[h], axis=0, keepdims=True) * norm
        dot_t[...] = (grad_t * norm).astype(jnp.bfloat16)
        dqt[...] = jnp.zeros_like(dqt)

        def chunk(d, carry):
            at = lax.rem(seq + d, 8)
            rows = strip(at, 256)
            expo = tokens[h * 8 + at]
            grad_probs = dot_nt(wu[rows, head], do[:, head])
            hidden[...] = (expo.astype(jnp.float32) * (grad_probs - delta)).astype(jnp.bfloat16)
            wu[rows, head] = dot_nt(expo, dot_t[...]).astype(jnp.bfloat16)
            wg[rows, key_lanes(h)] = (dot_nt(hidden[...], wd[key_lanes(h), :]) * scale).astype(jnp.bfloat16)
            dqt[...] += dot(wd[lanes(h), rows], hidden[...])

            @pl.when(d > 0)
            def _():
                out_copy(h, 1, d).start()
                out_copy(h, 2, d).start()

            return carry

        lax.fori_loop(0, 4, chunk, 0)
        lax.fori_loop(4, 8, chunk, 0)
        wg[:, head] = (dqt[...] * (norm * scale)).T.astype(jnp.bfloat16)
        for d in range(1, 8):
            out_copy(h, 0, d).start()
        for n in range(3):
            out_own(h, n).start()
    ag_step(4)

    sib_copy(3).wait_send()
    for copy in gh_copies:
        copy.wait_send()
    for n in range(6):
        z_copy(n).wait_send()
    for p in range(4):
        for i in range(4):
            rs_copy(p, i).wait_send()
            for m in range(3):
                ag_copy(p, i, m).wait_send()
    gh_store.wait()
    for h in range(2):
        for n in range(3):
            out_own(h, n).wait()
            for d in range(1, 8):
                out_copy(h, n, d).wait()


def layer(*arrays):
    dma = pltpu.SemaphoreType.DMA
    bf16, f32 = jnp.bfloat16, jnp.float32
    shapes = [(256, 2048)] * 4 + [(1, 2048, 512)] * 2 + [(1, 512, 2048)] + [(2048, 256)] * 3
    vmem = [
        ((16, 256, 2048), bf16), ((8, 8, 256), f32),
        ((2048, 512), bf16), ((2048, 512), bf16), ((512, 2048), bf16),
        ((8, 256), f32), ((8, 256), f32),
        ((8, 128, 256), bf16), ((8, 128, 256), bf16), ((8, 256, 128), bf16),
        ((4, 256, 2048), bf16), ((2, 2, 256, 512), f32),
        ((256, 2048), bf16), ((256, 512), bf16), ((256, 512), bf16), ((256, 512), bf16),
        ((256, 2048), bf16), ((2, 256, 2048), bf16), ((4, 16, 96, 512), bf16),
        ((4, 256, 2048), bf16), ((2, 2, 128, 2048), bf16), ((2, 128, 2048), bf16),
        ((4, 15, 96, 512), bf16), ((4, 96, 512), bf16), ((2048, 256), bf16),
        ((2, HD, 2048), f32), ((2, 1, 2048), f32), ((HD, 2048), bf16), ((HD, 2048), f32),
    ]
    sems = [
        (28,), (28,), (10,), (8,), (8,), (3, 8), (3, 8), (3,),
        (4,), (4,), (6,), (6,), (4, 4), (4, 4), (4, 4, 3), (4, 4, 3),
        (8,), (8,), (), (2, 3, 8), (2, 3, 8), (2, 3), (), (4, 3),
    ]
    return pl.pallas_call(
        layer_kernel,
        out_shape=[jax.ShapeDtypeStruct(shape, bf16) for shape in shapes],
        in_specs=[ANY] * len(arrays),
        out_specs=[ANY] * len(shapes),
        scratch_shapes=[pltpu.VMEM(*kind) for kind in vmem] + [dma(s) if s else dma for s in sems],
        compiler_params=pltpu.CompilerParams(
            collective_id=1, has_side_effects=True, vmem_limit_bytes=63 << 20
        ),
        name="layer",
    )(*arrays)


def finish_kernel(*refs):
    count = (len(refs) - 2) // 3
    srcs, dsts, bufs = refs[:count], refs[count : 2 * count], refs[2 * count : 3 * count]
    read_sem, write_sem = refs[3 * count :]
    reads = [pltpu.make_async_copy(src, buf, read_sem.at[n]) for n, (src, buf) in enumerate(zip(srcs, bufs))]
    writes = [pltpu.make_async_copy(buf, dst, write_sem.at[n]) for n, (buf, dst) in enumerate(zip(bufs, dsts))]
    for read in reads:
        read.start()
    for read, write in zip(reads, writes):
        read.wait()
        write.start()
    for write in writes:
        write.wait()


def finish(arrays):
    count = len(arrays)
    return pl.pallas_call(
        finish_kernel,
        out_shape=[jax.ShapeDtypeStruct(a.shape, a.dtype) for a in arrays],
        in_specs=[ANY] * count,
        out_specs=[ANY] * count,
        scratch_shapes=[pltpu.VMEM(a.shape, a.dtype) for a in arrays]
        + [pltpu.SemaphoreType.DMA((count,)), pltpu.SemaphoreType.DMA((count,))],
        compiler_params=pltpu.CompilerParams(vmem_limit_bytes=62 << 20),
        name="finish",
    )(*arrays)


def shards(
    attn_query, attn_key, attn_value, moe_input, cotangent,
    routes, route_weight, w_gate, w_up, w_down,
):
    expert_ids = jnp.arange(8, dtype=jnp.int32)
    hits = routes.T[:, None, :] == expert_ids[None, :, None]
    table = jnp.sum(
        jnp.where(hits, route_weight.astype(jnp.float32).T[:, None, :], 0.0), axis=0
    )
    results = layer(
        moe_input, cotangent, table, attn_query, attn_key, attn_value, w_gate, w_up, w_down
    )
    return tuple(finish(results[:7]))


def solution(mesh):
    tokens = P(("dp", "expert", "seq"), None)
    weights = P("expert", None, None)
    return jax.shard_map(
        shards,
        mesh=mesh,
        in_specs=(tokens,) * 7 + (weights,) * 3,
        out_specs=(tokens,) * 4 + (weights,) * 3,
        check_vma=False,
    )
```
